256 devices in a mesh: tm: 8 (over x, y_hi), space: 32 (over y_lo, z, core).
Axes of the slice: x: 4, y: 4 (y_hi: 2, y_lo: 2; y = y_hi * 2 + y_lo), z: 8, core: 2. Of those that a mesh axis runs over, the one named last changes fastest.
Arguments:
- snapshots: bfloat16 [4096, 65536], P('tm', 'space'), may hold values from -13 to 13
- modes_basis: bfloat16 [65536, 64], P('space'), may hold values from -0.0234375 to 0.0234375
- reg_weights: float32 [2144], replicated, may hold values from 0.3 to 3
Outputs:
- reduced: float32 [4096, 64], P('tm')
- time_rates: float32 [4096, 64], P('tm')
- normal: float32 [2144, 2144], P('tm', 'space')
- right_side: float32 [2144, 64], P('tm')
The draws below stay inside these ranges and needn't reach their ends.
All inputs are finite; a program needn't handle non-finite values.
Results may differ from the reference program's by a relative error of at most 0.0043.
Values sent between devices are 32-bit elements; how exact they have to be, the bound alone decides.
A program may use at most 128 MiB of HBM per device.

```python
import math
import jax
import jax.numpy as jnp

R = 64
FEATURES = 2144
SNAPS = 4096
NSTATE = 65536


def draw_snapshots(key, part):
    key = jax.random.fold_in(key, 11)
    key_rows, key_cols, key_noise = jax.random.split(key, 3)
    row_scale = jnp.exp(jax.random.uniform(key_rows, (SNAPS, 1), jnp.float32, math.log(0.6), math.log(1.6)))
    col_scale = jnp.exp(jax.random.uniform(key_cols, (1, NSTATE), jnp.float32, math.log(0.6), math.log(1.6)))
    field = jnp.clip(jax.random.normal(key_noise, (SNAPS, NSTATE), jnp.float32), -5.0, 5.0)
    return (row_scale * col_scale * field).astype(jnp.bfloat16)


def block_scale(own_key, extent, cuts, smallest, largest):
    gain = 1.0
    for dim, shards_of in cuts:
        steps = jax.random.uniform(jax.random.fold_in(jax.random.fold_in(own_key, 6), dim), (shards_of,), jnp.float32, smallest / len(cuts), largest / len(cuts))
        gain = gain * jnp.repeat(jnp.exp(steps), extent[dim] // shards_of).reshape((-1,) + (1,) * (len(extent) - 1 - dim))
    return gain


def bell_draw(own_key, shape, width, most, cuts=(), dtype=jnp.bfloat16):
    factor_of = block_scale(own_key, shape, cuts, -0.22, 0.18) if cuts else 1.0
    drawn = jax.random.normal(own_key, shape, jnp.float32) * width * factor_of
    return jnp.minimum(jnp.maximum(drawn, -most), most).astype(dtype)


def setup_inputs(seed: int = 0) -> dict:
    arg_keys = jax.random.split(jax.random.key(seed), 4)
    snapshots = draw_snapshots(jax.random.fold_in(arg_keys[3], 71), 0)
    modes_basis = bell_draw(arg_keys[1], (NSTATE, R), NSTATE ** -0.5, 0.0234375, ((0, 32),))
    reg_weights = jnp.clip(jnp.exp(jax.random.uniform(arg_keys[2], (FEATURES,), jnp.float32, math.log(0.3), math.log(3.0))), 0.3, 3.0)
    return dict(snapshots=snapshots, modes_basis=modes_basis, reg_weights=reg_weights)


def features_of(reduced):
    pieces = [reduced]
    for column in range(reduced.shape[1]):
        pieces.append(reduced[:, column:column + 1] * reduced[:, column:])
    return jnp.concatenate(pieces, axis=1).astype(jnp.bfloat16)


def rates_of(reduced):
    central = (reduced[2:] - reduced[:-2]) * 0.5
    first_row = reduced[1:2] - reduced[0:1]
    last_row = reduced[-1:] - reduced[-2:-1]
    return jnp.concatenate([first_row, central, last_row], axis=0)


def reference(snapshots, modes_basis, reg_weights):
    reduced = jnp.dot(snapshots, modes_basis, preferred_element_type=jnp.float32)
    time_rates = rates_of(reduced)
    features = features_of(reduced)
    rates_bf = time_rates.astype(jnp.bfloat16)
    inv_count = 1.0 / SNAPS
    normal = jnp.dot(features.T, features, preferred_element_type=jnp.float32) * inv_count + jnp.diag(reg_weights)
    right_side = jnp.dot(features.T, rates_bf, preferred_element_type=jnp.float32) * inv_count
    return (reduced, time_rates, normal, right_side)
```

```python
import functools

import jax
import jax.numpy as jnp
from jax import lax
from jax.experimental import pallas as pl
from jax.experimental.pallas import tpu as pltpu
from jax.sharding import PartitionSpec as P

MESH = pl.DeviceIdType.MESH
F32 = jnp.float32
BF16 = jnp.bfloat16
CONTRACT = (((1,), (1,)), ((), ()))

NX, NY, NZ = 4, 4, 8
R = 64
FEATURES = 2144
SNAPS = 4096
GROUP = 512
LANES = 128
KB = GROUP // LANES
HALF = 256
ROWS = FEATURES // 8
COLS = FEATURES // 32
ROWS_P = 272
COLS_8 = 72
COLS_P = 2 * COLS_8
WIDE = 384
SEL = ROWS_P + COLS_P
OUT_N = COLS_P + R


def start_of(q):
    return R + R * q - (q * (q - 1)) // 2


def position():
    t, s = lax.axis_index("tm"), lax.axis_index("space")
    x, yh = t // 2, t % 2
    yl, z, c = s // 16, (s % 16) // 2, s % 2
    return t, s, x, yh * 2 + yl, z, c


def device_at(x, y, z, c):
    return (x * 2 + y // 2, (y % 2) * 16 + z * 2 + c)


def selectors(t, s, sel_ref):
    shape = (SEL, 256)
    row = lax.broadcasted_iota(jnp.int32, shape, 0)
    lane = lax.broadcasted_iota(jnp.int32, shape, 1)
    column = row - ROWS_P
    column = jnp.where(column < COLS_8, column, column - COLS_8 + COLS)
    f = jnp.where(row < ROWS_P, ROWS * t + row, 2 * COLS * (s // 2) + column)
    q = lane % R
    part = lane < 3 * R
    begin = start_of(q)
    linear = f < R
    first = (f >= begin) & (f < start_of(q + 1))
    first = ((linear & (f == q)) | first) & part
    count = jnp.sum(jnp.where((f >= begin) & (lane < R), 1.0, 0.0), axis=1, keepdims=True)
    i = count.astype(jnp.int32) - 1
    j = f - start_of(i) + i
    second = (linear & (lane == 3 * R)) | (~linear & (q == j) & part)
    sel_ref[:SEL, :] = jnp.where(first, 1.0, 0.0).astype(BF16)
    sel_ref[SEL:, :] = jnp.where(second, 1.0, 0.0).astype(BF16)


def kernel(
    snap_hbm, basis_hbm, reg_hbm,
    red_ref, rate_ref, norm_ref, rhs_ref,
    snap_v, basis_v, reg_s, pbuf, rbuf, gbuf, sel, edge, oedge, rates, acc, oacc, norm_v, rhs_v,
    in_sem, rs_send, rs_recv, g1_send, g1_recv, g2_send, g2_recv, g3_send, g3_recv, x_send, x_recv, out_sem,
):
    t, s, x, y, z, c = position()
    yl = y % 2
    me = 4 * x + y
    other = device_at(x, y, z, 1 - c)

    basis_in = pltpu.make_async_copy(basis_hbm, basis_v, in_sem.at[KB])
    basis_in.start()
    snaps_in = []
    for kb in range(KB):
        rows = pl.ds(kb * LANES, LANES)
        copy = pltpu.make_async_copy(snap_hbm.at[rows], snap_v.at[rows], in_sem.at[kb])
        copy.start()
        snaps_in.append(copy)
    reg_in = pltpu.make_async_copy(reg_hbm, reg_s, in_sem.at[KB + 1])
    reg_in.start()

    barrier = pltpu.get_barrier_semaphore()
    for d in range(1, 32):
        pl.semaphore_signal(barrier, inc=1, device_id=(t, (s + d) % 32), device_id_type=MESH)
    for d in range(1, NX):
        pl.semaphore_signal(barrier, inc=1, device_id=device_at((x + d) % NX, y, z, c), device_id_type=MESH)
    for d in range(2):
        pl.semaphore_signal(
            barrier, inc=1, device_id=device_at(x, (y // 2 * 2 + 2) % 4 + d, z, c), device_id_type=MESH
        )

    basis_in.wait()
    for kb in range(KB):
        snaps_in[kb].wait()
        pbuf[kb] = lax.dot_general(
            basis_v[...], snap_v[kb * LANES:(kb + 1) * LANES, :], CONTRACT, preferred_element_type=F32
        )
        if kb == 0:
            pl.semaphore_wait(barrier, 36)
        for d in range(NZ):
            zz = (z + d) % NZ
            to = (kb % 2) * 16 + zz * 2 + kb // 2
            copy = pltpu.make_async_remote_copy(
                src_ref=pbuf.at[kb, pl.ds(pl.multiple_of(8 * zz, 8), 8)],
                dst_ref=rbuf.at[(s - to + 32) % 32],
                send_sem=rs_send, recv_sem=rs_recv,
                device_id=(t, to), device_id_type=MESH,
            )
            if d == 0:
                pl.when(to != s)(copy.start)
            else:
                copy.start()

    selectors(t, s, sel)
    reg_in.wait()

    pltpu.make_async_remote_copy(
        src_ref=rbuf.at[pl.ds(1, 31)], dst_ref=rbuf.at[pl.ds(1, 31)],
        send_sem=rs_send, recv_sem=rs_recv, device_id=other, device_id_type=MESH,
    ).wait()
    zrows = pl.ds(pl.multiple_of(8 * z, 8), 8)
    total = pbuf[2 * c + yl, zrows, :]
    for d in range(1, 32):
        total = total + rbuf[d]
    gbuf[me, zrows, :] = total

    for d in range(1, NZ):
        pltpu.make_async_remote_copy(
            src_ref=gbuf.at[me, zrows], dst_ref=gbuf.at[me, zrows],
            send_sem=g1_send, recv_sem=g1_recv,
            device_id=device_at(x, y, (z + d) % NZ, c), device_id_type=MESH,
        ).start()
    pltpu.make_async_remote_copy(
        src_ref=gbuf.at[me, pl.ds(0, 56)], dst_ref=gbuf.at[me, pl.ds(0, 56)],
        send_sem=g1_send, recv_sem=g1_recv, device_id=other, device_id_type=MESH,
    ).wait()

    def along_x(ref, d, sems):
        return pltpu.make_async_remote_copy(
            src_ref=ref, dst_ref=ref, send_sem=sems[0], recv_sem=sems[1],
            device_id=device_at((x + d) % NX, y, z, c), device_id_type=MESH,
        )

    def along_y(ref, d, sems):
        return pltpu.make_async_remote_copy(
            src_ref=ref, dst_ref=ref, send_sem=sems[0], recv_sem=sems[1],
            device_id=device_at(x, (y + d) % NY, z, c), device_id_type=MESH,
        )

    first_hop = []
    for d in (1, 3, 2):
        for k, along in enumerate((along_x, along_y)):
            copy = along(gbuf.at[me], d, (g2_send.at[k, d], g2_recv.at[k, d]))
            copy.start()
            first_hop.append(copy)
    for d in (1, 3, 2):
        along_x(gbuf.at[me], d, (g2_send.at[0, d], g2_recv.at[0, d])).wait_recv()
        source = 4 * ((x - d + NX) % NX) + y
        for e in (1, 3, 2):
            along_y(gbuf.at[source, pl.ds(0, 32)], e, (g3_send, g3_recv)).start()
        along_y(gbuf.at[me], d, (g2_send.at[1, d], g2_recv.at[1, d])).wait_recv()
        source = 4 * x + (y - d + NY) % NY
        for e in (1, 3, 2):
            along_x(gbuf.at[source, pl.ds(32, 32)], e, (g3_send, g3_recv)).start()
    for copy in first_hop:
        copy.wait_send()
    along_x(gbuf.at[pl.ds(0, 9)], 1, (g3_send, g3_recv)).wait()

    def across(src, dst, k):
        return pltpu.make_async_remote_copy(
            src_ref=src, dst_ref=dst, send_sem=x_send.at[k], recv_sem=x_recv.at[k],
            device_id=other, device_id_type=MESH,
        )

    lane = lax.broadcasted_iota(jnp.int32, (R, LANES), 1)
    edges = jnp.zeros((R, LANES), F32)
    for g in range(8):
        edges = jnp.where(lane == 2 * g, gbuf[2 * g][:, 0:1], edges)
        edges = jnp.where(lane == 2 * g + 1, gbuf[2 * g + 1][:, LANES - 1:], edges)
    edge[...] = edges
    send_edge = across(edge, oedge, 0)
    send_edge.start()
    outs = []
    for h in range(2):
        mine = red_ref.at[:, pl.ds(pl.multiple_of(c * HALF + h * LANES, LANES), LANES)]
        copy = across(gbuf.at[2 * t + h], mine, 1 + h)
        copy.start()
        outs.append(copy)
        copy = pltpu.make_async_copy(gbuf.at[2 * t + h], mine, out_sem.at[h])
        copy.start()
        outs.append(copy)
    send_edge.wait()

    got = oedge[...]
    left = jnp.where(c == 0, pltpu.roll(got, 2, 1), got)
    right = jnp.where(c == 0, got, pltpu.roll(got, LANES - 2, 1))
    lane = lax.broadcasted_iota(jnp.int32, (R, HALF), 1)
    for g in range(8):
        r = jnp.concatenate([gbuf[2 * g], gbuf[2 * g + 1]], axis=1)
        before = jnp.where(lane == 0, left[:, 2 * g + 1:2 * g + 2], pltpu.roll(r, 1, 1))
        after = jnp.where(lane == HALF - 1, right[:, 2 * g:2 * g + 1], pltpu.roll(r, HALF - 1, 1))
        rate = (after - before) * 0.5
        if g == 0:
            rate = jnp.where((lane == 0) & (c == 0), after - r, rate)
        if g == 7:
            rate = jnp.where((lane == HALF - 1) & (c == 1), r - before, rate)
        rates[g] = rate
    mine = rate_ref.at[:, pl.ds(pl.multiple_of(c * HALF, HALF), HALF)]
    copy = across(rates.at[t], mine, 3)
    copy.start()
    outs.append(copy)
    copy = pltpu.make_async_copy(rates.at[t], mine, out_sem.at[2])
    copy.start()
    outs.append(copy)

    acc[...] = jnp.zeros_like(acc)
    ones = jnp.where(lax.broadcasted_iota(jnp.int32, (R, HALF), 0) == 0, 1.0, 0.0).astype(BF16)

    def products(g, carry):
        r = jnp.concatenate([gbuf[2 * g], gbuf[2 * g + 1]], axis=1)
        high = r.astype(BF16)
        rest = r - high.astype(F32)
        middle = rest.astype(BF16)
        low = (rest - middle.astype(F32)).astype(BF16)
        parts = jnp.concatenate([high, middle, low, ones], axis=0)
        picked = jnp.dot(sel[...], parts, preferred_element_type=F32)
        feature = (picked[:SEL] * picked[SEL:]).astype(BF16)
        columns = jnp.concatenate([feature[ROWS_P:], rates[g].astype(BF16)], axis=0)
        acc[:, :ROWS_P] += lax.dot_general(
            columns, feature[:ROWS_P], CONTRACT, preferred_element_type=F32
        )
        return carry

    lax.fori_loop(0, 8, products, 0)
    theirs = pl.ds(pl.multiple_of((1 - c) * COLS_8, 8), COLS_8)
    send_norm = across(acc.at[theirs], oacc.at[pl.ds(0, COLS_8)], 4)
    send_norm.start()
    send_rhs = across(acc.at[pl.ds(COLS_P, R)], oacc.at[pl.ds(COLS_8, R)], 5)
    send_rhs.start()

    spot = COLS * (s % 4)
    lane = lax.broadcasted_iota(jnp.int32, (8, WIDE), 1)

    def pick_weight(i, v):
        return jnp.where(lane == spot + i, reg_s[COLS * s + i], v)

    weight = lax.fori_loop(0, COLS, pick_weight, jnp.zeros((8, WIDE), F32))
    column = lax.broadcasted_iota(jnp.int32, (COLS, ROWS), 0)
    row = lax.broadcasted_iota(jnp.int32, (COLS, ROWS), 1)
    diagonal = (ROWS * t + row) == (COLS * s + column)

    send_norm.wait()
    mine = pl.ds(pl.multiple_of(c * COLS_8, 8), COLS_8)
    summed = (acc[mine, :] + oacc[:COLS_8, :]) * (1.0 / SNAPS)
    norm_v[...] = summed[:COLS, :ROWS] + jnp.where(diagonal, weight[0:1, :ROWS], 0.0)
    copy = pltpu.make_async_copy(norm_v, norm_ref, out_sem.at[3])
    copy.start()
    outs.append(copy)
    send_rhs.wait()
    summed = (acc[COLS_P:, :] + oacc[COLS_8:, :]) * (1.0 / SNAPS)
    rhs_v[...] = summed[:, :ROWS]
    copy = pltpu.make_async_copy(rhs_v, rhs_ref, out_sem.at[4])
    copy.start()
    outs.append(copy)
    for copy in outs:
        copy.wait()


def local(snapshots, modes_basis, reg_weights):
    f32 = lambda *shape: pltpu.VMEM(shape, F32)
    dma = pltpu.SemaphoreType.DMA
    outs = pl.pallas_call(
        kernel,
        out_shape=(
            jax.ShapeDtypeStruct((R, GROUP), F32),
            jax.ShapeDtypeStruct((R, GROUP), F32),
            jax.ShapeDtypeStruct((COLS, ROWS), F32),
            jax.ShapeDtypeStruct((R, ROWS), F32),
        ),
        in_specs=[pl.BlockSpec(memory_space=pltpu.HBM)] * 3,
        out_specs=[pl.BlockSpec(memory_space=pltpu.HBM)] * 4,
        scratch_shapes=[
            pltpu.VMEM((GROUP, 2048), BF16),
            pltpu.VMEM((R, 2048), BF16),
            pltpu.SMEM((FEATURES,), F32),
            f32(KB, R, LANES),
            f32(32, 8, LANES),
            f32(16, R, LANES),
            pltpu.VMEM((2 * SEL, 256), BF16),
            f32(R, LANES),
            f32(R, LANES),
            f32(8, R, HALF),
            f32(OUT_N, WIDE),
            f32(COLS_8 + R, WIDE),
            f32(COLS, ROWS),
            f32(R, ROWS),
            dma((KB + 2,)),
            dma, dma,
            dma, dma,
            dma((2, 4)), dma((2, 4)),
            dma, dma,
            dma((6,)), dma((6,)),
            dma((5,)),
        ],
        compiler_params=pltpu.CompilerParams(
            collective_id=0, has_side_effects=True, vmem_limit_bytes=32 * 1024 * 1024
        ),
        cost_estimate=pl.CostEstimate(flops=1 << 30, bytes_accessed=3 << 20, transcendentals=0),
    )(snapshots, modes_basis.T, reg_weights)
    return tuple(out.T for out in outs)


def solution(mesh):
    return jax.shard_map(
        local,
        mesh=mesh,
        in_specs=(P("tm", "space"), P("space", None), P()),
        out_specs=(P("tm", None), P("tm", None), P("tm", "space"), P("tm", None)),
        check_vma=False,
    )
```

```python
import functools

import jax
import jax.numpy as jnp
from jax import lax
from jax.experimental import pallas as pl
from jax.experimental.pallas import tpu as pltpu
from jax.sharding import PartitionSpec as P

MESH = pl.DeviceIdType.MESH
F32 = jnp.float32
BF16 = jnp.bfloat16
CONTRACT = (((1,), (1,)), ((), ()))

NX, NY, NZ = 4, 4, 8
R = 64
FEATURES = 2144
SNAPS = 4096
GROUP = 512
LANES = 128
KB = GROUP // LANES
HALF = 256
ROWS = FEATURES // 8
COLS = FEATURES // 32
ROWS_P = 272
COLS_8 = 72
COLS_P = 2 * COLS_8
WIDE = 384
SEL = ROWS_P + COLS_P
XY_ORDER = [(dx, dy) for dx in (0, 1, 3, 2) for dy in (0, 1, 3, 2) if dx or dy]
Z_ORDER = (1, 7, 2, 6, 3, 5, 4)


def start_of(q):
    return R + R * q - (q * (q - 1)) // 2


def position():
    t, s = lax.axis_index("tm"), lax.axis_index("space")
    x, yh = t // 2, t % 2
    yl, z, c = s // 16, (s % 16) // 2, s % 2
    return t, s, x, yh * 2 + yl, z, c


def device_at(x, y, z, c):
    return (x * 2 + y // 2, (y % 2) * 16 + z * 2 + c)


def selectors(t, s, sel_ref):
    shape = (SEL, 256)
    row = lax.broadcasted_iota(jnp.int32, shape, 0)
    lane = lax.broadcasted_iota(jnp.int32, shape, 1)
    column = row - ROWS_P
    column = jnp.where(column < COLS_8, column, column - COLS_8 + COLS)
    f = jnp.where(row < ROWS_P, ROWS * t + row, 2 * COLS * (s // 2) + column)
    q = lane % R
    part = lane < 3 * R
    begin = start_of(q)
    linear = f < R
    first = (f >= begin) & (f < start_of(q + 1))
    first = ((linear & (f == q)) | first) & part
    count = jnp.sum(jnp.where((f >= begin) & (lane < R), 1.0, 0.0), axis=1, keepdims=True)
    i = count.astype(jnp.int32) - 1
    j = f - start_of(i) + i
    second = (linear & (lane == 3 * R)) | (~linear & (q == j) & part)
    sel_ref[:SEL, :] = jnp.where(first, 1.0, 0.0).astype(BF16)
    sel_ref[SEL:, :] = jnp.where(second, 1.0, 0.0).astype(BF16)


def kernel(
    snap_hbm, basis_hbm, reg_hbm,
    red_ref, rate_ref, norm_ref, rhs_ref,
    snap_v, basis_v, reg_s, pbuf, rbuf, gbuf, obuf, sel, rates, rates_bf, feats, acc, rhs, oacc,
    in_sem, rs_send, rs_recv, g1_send, g1_recv, g2_send, g2_recv, f_send, f_recv, x_send, x_recv, out_sem,
):
    t, s, x, y, z, c = position()
    yl = y % 2
    me = 4 * x + y
    other = device_at(x, y, z, 1 - c)

    basis_in = pltpu.make_async_copy(basis_hbm, basis_v, in_sem.at[KB])
    basis_in.start()
    snaps_in = []
    for kb in range(KB):
        rows = pl.ds(kb * LANES, LANES)
        copy = pltpu.make_async_copy(snap_hbm.at[rows], snap_v.at[rows], in_sem.at[kb])
        copy.start()
        snaps_in.append(copy)
    reg_in = pltpu.make_async_copy(reg_hbm, reg_s, in_sem.at[KB + 1])
    reg_in.start()

    barrier = pltpu.get_barrier_semaphore()
    for d in range(1, 32):
        pl.semaphore_signal(barrier, inc=1, device_id=(t, (s + d) % 32), device_id_type=MESH)
    for dx in range(NX):
        for dy in range(NY):
            peer = device_at((x + dx) % NX, (y + dy) % NY, z, c)
            if dx:
                pl.semaphore_signal(barrier, inc=1, device_id=peer, device_id_type=MESH)
    for d in range(2):
        pl.semaphore_signal(
            barrier, inc=1, device_id=device_at(x, (y // 2 * 2 + 2) % 4 + d, z, c), device_id_type=MESH
        )

    basis_in.wait()
    for kb in range(KB):
        snaps_in[kb].wait()
        pbuf[kb] = lax.dot_general(
            basis_v[...], snap_v[kb * LANES:(kb + 1) * LANES, :], CONTRACT, preferred_element_type=F32
        )
        if kb == 0:
            pl.semaphore_wait(barrier, 31 + 12 + 2)
        for d in range(NZ):
            zz = (z + d) % NZ
            to = (kb % 2) * 16 + zz * 2 + kb // 2
            copy = pltpu.make_async_remote_copy(
                src_ref=pbuf.at[kb, pl.ds(pl.multiple_of(8 * zz, 8), 8)],
                dst_ref=rbuf.at[(s - to + 32) % 32],
                send_sem=rs_send, recv_sem=rs_recv,
                device_id=(t, to), device_id_type=MESH,
            )
            if d == 0:
                pl.when(to != s)(copy.start)
            else:
                copy.start()

    reg_in.wait()
    selectors(t, s, sel)

    spot = COLS * (s % 4)
    lane = lax.broadcasted_iota(jnp.int32, (8, WIDE), 1)

    def pick_weight(i, v):
        return jnp.where(lane == spot + i, reg_s[COLS * s + i], v)

    weight = lax.fori_loop(0, COLS, pick_weight, jnp.zeros((8, WIDE), F32))
    acc[...] = jnp.zeros_like(acc)

    pltpu.make_async_remote_copy(
        src_ref=rbuf.at[pl.ds(1, 31)], dst_ref=rbuf.at[pl.ds(1, 31)],
        send_sem=rs_send, recv_sem=rs_recv, device_id=other, device_id_type=MESH,
    ).wait()
    zrows = pl.ds(pl.multiple_of(8 * z, 8), 8)
    total = pbuf[2 * c + yl, zrows, :]
    for d in range(1, 32):
        total = total + rbuf[d]
    gbuf[me, zrows, :] = total

    def tile(zz):
        return gbuf.at[me, pl.ds(pl.multiple_of(8 * zz, 8), 8)]

    def along_z(d):
        return pltpu.make_async_remote_copy(
            src_ref=tile(z), dst_ref=tile(z), send_sem=g1_send, recv_sem=g1_recv.at[d],
            device_id=device_at(x, y, (z + d) % NZ, c), device_id_type=MESH,
        )

    def over_xy(zz):
        for dx, dy in XY_ORDER:
            pltpu.make_async_remote_copy(
                src_ref=tile(zz), dst_ref=tile(zz), send_sem=g2_send, recv_sem=g2_recv.at[4 * dx + dy],
                device_id=device_at((x + dx) % NX, (y + dy) % NY, z, c), device_id_type=MESH,
            ).start()

    for d in Z_ORDER:
        along_z(d).start()
    over_xy(z)
    for d in Z_ORDER:
        along_z(d).wait_recv()
        over_xy((z - d + NZ) % NZ)
    pltpu.make_async_remote_copy(
        src_ref=gbuf.at[me, pl.ds(0, 56)], dst_ref=gbuf.at[me, pl.ds(0, 56)],
        send_sem=g1_send, recv_sem=g1_recv.at[0], device_id=other, device_id_type=MESH,
    ).wait_send()

    def across(src, dst, sems):
        return pltpu.make_async_remote_copy(
            src_ref=src, dst_ref=dst, send_sem=sems[0], recv_sem=sems[1],
            device_id=other, device_id_type=MESH,
        )

    ones = jnp.where(lax.broadcasted_iota(jnp.int32, (R, HALF), 0) == 0, 1.0, 0.0).astype(BF16)

    def products(n, carry):
        k = n // 2
        dx = k + k // 2 - 2 * (k // 3)
        xx = (x - dx + NX) % NX
        yh = (y // 2 + n) % 2
        for h in range(2):
            dy = (y - 2 * yh - h + NY) % NY
            source = 4 * xx + 2 * yh + h
            arrived = pltpu.make_async_remote_copy(
                src_ref=gbuf.at[source], dst_ref=gbuf.at[source], send_sem=g2_send, recv_sem=g2_recv.at[4 * dx + dy],
                device_id=other, device_id_type=MESH,
            )
            pl.when(source != me)(arrived.wait_recv)
        g = 2 * xx + yh
        both = pl.ds(2 * g, 2)
        across(gbuf.at[both], obuf.at[both], (f_send, f_recv)).start()
        r = jnp.concatenate([gbuf[2 * g], gbuf[2 * g + 1]], axis=1)
        rates[g] = (pltpu.roll(r, HALF - 1, 1) - pltpu.roll(r, 1, 1)) * 0.5
        high = r.astype(BF16)
        rest = r - high.astype(F32)
        middle = rest.astype(BF16)
        low = (rest - middle.astype(F32)).astype(BF16)
        parts = jnp.concatenate([high, middle, low, ones], axis=0)
        picked = jnp.dot(sel[...], parts, preferred_element_type=F32)
        feature = (picked[:SEL] * picked[SEL:]).astype(BF16)
        feats[:, pl.ds(pl.multiple_of(g * HALF, HALF), HALF)] = feature[:ROWS_P]
        acc[:, :ROWS_P] += lax.dot_general(
            feature[ROWS_P:], feature[:ROWS_P], CONTRACT, preferred_element_type=F32
        )
        return carry

    lax.fori_loop(0, 8, products, 0)
    theirs = pl.ds(pl.multiple_of((1 - c) * COLS_8, 8), COLS_8)
    send_norm = across(acc.at[theirs], oacc.at[pl.ds(0, COLS_8)], (x_send.at[0], x_recv.at[0]))
    send_norm.start()
    pltpu.make_async_remote_copy(
        src_ref=gbuf.at[pl.ds(0, 15)], dst_ref=gbuf.at[pl.ds(0, 15)],
        send_sem=g2_send, recv_sem=g1_recv.at[0], device_id=other, device_id_type=MESH,
    ).wait_send()

    across(gbuf, obuf, (f_send, f_recv)).wait()
    lane = lax.broadcasted_iota(jnp.int32, (R, LANES), 1)

    def edges(g, carry):
        low, high = gbuf[2 * g], gbuf[2 * g + 1]
        before = pltpu.roll(obuf[(2 * g - 1 + 2 * c + 16) % 16], 1, 1)
        after = pltpu.roll(obuf[(2 * g + 2 * c) % 16], LANES - 1, 1)
        second = pltpu.roll(low, LANES - 1, 1)
        last = pltpu.roll(high, 1, 1)
        first_rate = jnp.where((g == 0) & (c == 0), second - low, (second - before) * 0.5)
        last_rate = jnp.where((g == 7) & (c == 1), high - last, (after - last) * 0.5)
        first_rate = jnp.where(lane == 0, first_rate, rates[g, :, :LANES])
        last_rate = jnp.where(lane == LANES - 1, last_rate, rates[g, :, LANES:])
        rates[g, :, :LANES] = first_rate
        rates[g, :, LANES:] = last_rate
        start = pl.multiple_of(g * HALF, HALF)
        rates_bf[:, pl.ds(start, LANES)] = first_rate.astype(BF16)
        rates_bf[:, pl.ds(start + LANES, LANES)] = last_rate.astype(BF16)
        return carry

    lax.fori_loop(0, 8, edges, 0)
    rhs[:, :ROWS_P] = lax.dot_general(rates_bf[...], feats[...], CONTRACT, preferred_element_type=F32)
    send_rhs = across(rhs, oacc.at[pl.ds(COLS_8, R)], (x_send.at[1], x_recv.at[1]))
    send_rhs.start()

    outs = []
    mine = pl.ds(pl.multiple_of(c * HALF, HALF), HALF)
    send_rate = across(rates.at[t], rate_ref.at[:, mine], (x_send.at[2], x_recv.at[2]))
    send_rate.start()
    copy = pltpu.make_async_copy(rates.at[t], rate_ref.at[:, mine], out_sem.at[0])
    copy.start()
    outs.append(copy)
    for h in range(2):
        for k, (buf, core) in enumerate(((gbuf, c), (obuf, 1 - c))):
            lanes = pl.ds(pl.multiple_of(core * HALF + h * LANES, LANES), LANES)
            copy = pltpu.make_async_copy(buf.at[2 * t + h], red_ref.at[:, lanes], out_sem.at[1 + 2 * h + k])
            copy.start()
            outs.append(copy)

    column = lax.broadcasted_iota(jnp.int32, (COLS, ROWS), 0)
    row = lax.broadcasted_iota(jnp.int32, (COLS, ROWS), 1)
    diagonal = (ROWS * t + row) == (COLS * s + column)
    send_norm.wait()
    summed = (acc[pl.ds(pl.multiple_of(c * COLS_8, 8), COLS_8), :] + oacc[:COLS_8, :]) * (1.0 / SNAPS)
    norm_ref[...] = summed[:COLS, :ROWS] + jnp.where(diagonal, weight[0:1, :ROWS], 0.0)
    send_rate.wait()
    for copy in outs:
        copy.wait()
    send_rhs.wait()
    summed = (rhs[...] + oacc[COLS_8:, :]) * (1.0 / SNAPS)
    rhs_ref[...] = summed[:, :ROWS]


def write(red, rate, norm, rhs, red_out, rate_out, norm_out, rhs_out, sem):
    pairs = ((red, red_out), (rate, rate_out), (norm, norm_out), (rhs, rhs_out))
    copies = [pltpu.make_async_copy(a, b, sem.at[k]) for k, (a, b) in enumerate(pairs)]
    for copy in copies:
        copy.start()
    for copy in copies:
        copy.wait()


def local(snapshots, modes_basis, reg_weights):
    f32 = lambda *shape: pltpu.VMEM(shape, F32)
    bf16 = lambda *shape: pltpu.VMEM(shape, BF16)
    dma = pltpu.SemaphoreType.DMA
    shapes = ((R, GROUP), (R, GROUP), (COLS, ROWS), (R, ROWS))
    in_hbm = lambda a: pltpu.with_memory_space_constraint(a, pltpu.HBM)
    in_vmem = lambda a: pltpu.with_memory_space_constraint(a, pltpu.VMEM)
    outs = pl.pallas_call(
        kernel,
        out_shape=tuple(f32(*shape) for shape in shapes),
        in_specs=[pl.BlockSpec(memory_space=pltpu.HBM)] * 3,
        out_specs=[pl.BlockSpec(memory_space=pltpu.VMEM)] * 4,
        scratch_shapes=[
            bf16(GROUP, 2048),
            bf16(R, 2048),
            pltpu.SMEM((FEATURES,), F32),
            f32(KB, R, LANES),
            f32(32, 8, LANES),
            f32(16, R, LANES),
            f32(16, R, LANES),
            bf16(2 * SEL, 256),
            f32(8, R, HALF),
            bf16(R, 8 * HALF),
            bf16(ROWS_P, 8 * HALF),
            f32(COLS_P, WIDE),
            f32(R, WIDE),
            f32(COLS_8 + R, WIDE),
            dma((KB + 2,)),
            dma, dma,
            dma, dma((NZ,)),
            dma, dma((16,)),
            dma, dma,
            dma((3,)), dma((3,)),
            dma((5,)),
        ],
        compiler_params=pltpu.CompilerParams(
            collective_id=0, has_side_effects=True, vmem_limit_bytes=32 * 1024 * 1024
        ),
        cost_estimate=pl.CostEstimate(flops=1 << 30, bytes_accessed=3 << 20, transcendentals=0),
    )(in_hbm(snapshots), in_hbm(modes_basis.T), in_hbm(reg_weights))
    outs = pl.pallas_call(
        write,
        out_shape=tuple(jax.ShapeDtypeStruct(shape, F32) for shape in shapes),
        in_specs=[pl.BlockSpec(memory_space=pltpu.VMEM)] * 4,
        out_specs=[pl.BlockSpec(memory_space=pltpu.HBM)] * 4,
        scratch_shapes=[dma((4,))],
        compiler_params=pltpu.CompilerParams(vmem_limit_bytes=4 * 1024 * 1024),
    )(*[in_vmem(out) for out in outs])
    return tuple(out.T for out in outs)


def solution(mesh):
    return jax.shard_map(
        local,
        mesh=mesh,
        in_specs=(P("tm", "space"), P("space", None), P()),
        out_specs=(P("tm", None), P("tm", None), P("tm", "space"), P("tm", None)),
        check_vma=False,
    )
```

```python
import functools

import jax
import jax.numpy as jnp
from jax import lax
from jax.experimental import pallas as pl
from jax.experimental.pallas import tpu as pltpu
from jax.sharding import PartitionSpec as P

MESH = pl.DeviceIdType.MESH
F32 = jnp.float32
BF16 = jnp.bfloat16
CONTRACT = (((1,), (1,)), ((), ()))

NX, NY, NZ = 4, 4, 8
R = 64
FEATURES = 2144
SNAPS = 4096
GROUP = 512
LANES = 128
HALF = 256
ROWS = FEATURES // 8
COLS = FEATURES // 32
ROWS_P = 272
COLS_8 = 72
COLS_P = 2 * COLS_8
WIDE = 384
SEL = ROWS_P + COLS_P
XY_ORDER = [(dx, dy) for dx in (0, 1, 3, 2) for dy in (0, 1, 3, 2) if dx or dy]
Z_ORDER = (1, 7, 2, 6, 3, 5, 4)


def start_of(q):
    return R + R * q - (q * (q - 1)) // 2


def position():
    t, s = lax.axis_index("tm"), lax.axis_index("space")
    x, yh = t // 2, t % 2
    yl, z, c = s // 16, (s % 16) // 2, s % 2
    return t, s, x, yh * 2 + yl, z, c


def device_at(x, y, z, c):
    return (x * 2 + y // 2, (y % 2) * 16 + z * 2 + c)


def selectors(t, s, sel_ref):
    shape = (SEL, 256)
    row = lax.broadcasted_iota(jnp.int32, shape, 0)
    lane = lax.broadcasted_iota(jnp.int32, shape, 1)
    column = row - ROWS_P
    column = jnp.where(column < COLS_8, column, column - COLS_8 + COLS)
    f = jnp.where(row < ROWS_P, ROWS * t + row, 2 * COLS * (s // 2) + column)
    q = lane % R
    part = lane < 3 * R
    begin = start_of(q)
    linear = f < R
    first = (f >= begin) & (f < start_of(q + 1))
    first = ((linear & (f == q)) | first) & part
    count = jnp.sum(jnp.where((f >= begin) & (lane < R), 1.0, 0.0), axis=1, keepdims=True)
    i = count.astype(jnp.int32) - 1
    j = f - start_of(i) + i
    second = (linear & (lane == 3 * R)) | (~linear & (q == j) & part)
    sel_ref[:SEL, :] = jnp.where(first, 1.0, 0.0).astype(BF16)
    sel_ref[SEL:, :] = jnp.where(second, 1.0, 0.0).astype(BF16)


def split3(r):
    high = r.astype(BF16)
    rest = r - high.astype(F32)
    middle = rest.astype(BF16)
    low = (rest - middle.astype(F32)).astype(BF16)
    ones = jnp.where(lax.broadcasted_iota(jnp.int32, r.shape, 0) == 0, 1.0, 0.0).astype(BF16)
    return jnp.concatenate([high, middle, low, ones], axis=0)


def slopes(r):
    width = r.shape[1]
    return (pltpu.roll(r, width - 1, 1) - pltpu.roll(r, 1, 1)) * 0.5


def kernel(
    snap_hbm, basis_hbm, reg_hbm,
    red_ref, rate_ref, norm_ref, rhs_ref,
    snap_v, basis_v, reg_s, xbuf, ybuf, pbuf, rbuf, gbuf, sel, edge, oedge, acc, oacc,
    in_sem, rs_send, rs_recv, g1_send, g1_recv, g2_send, g2_recv, x_send, x_recv,
):
    t, s, x, y, z, c = position()
    yl = y % 2
    me = 4 * x + y
    other = device_at(x, y, z, 1 - c)

    basis_in = pltpu.make_async_copy(basis_hbm, basis_v, in_sem.at[2])
    basis_in.start()
    snaps_in = []
    for h, core in enumerate((1 - c, c)):
        rows = pl.ds(pl.multiple_of(core * HALF, HALF), HALF)
        copy = pltpu.make_async_copy(snap_hbm.at[rows], snap_v.at[h], in_sem.at[h])
        copy.start()
        snaps_in.append(copy)
    reg_in = pltpu.make_async_copy(reg_hbm, reg_s, in_sem.at[3])
    reg_in.start()

    barrier = pltpu.get_barrier_semaphore()
    peers = [other]
    for d in range(1, 16):
        w = (s // 2 + d) % 16
        peers.append((t, 2 * w + c))
    for dx in range(1, NX):
        for dy in range(NY):
            peers.append(device_at((x + dx) % NX, (y + dy) % NY, z, c))
    for d in range(2):
        peers.append(device_at(x, (y // 2 * 2 + 2) % 4 + d, z, c))
    for peer in peers:
        pl.semaphore_signal(barrier, inc=1, device_id=peer, device_id_type=MESH)

    def across(src, dst, k):
        return pltpu.make_async_remote_copy(
            src_ref=src, dst_ref=dst, send_sem=x_send.at[k], recv_sem=x_recv.at[k],
            device_id=other, device_id_type=MESH,
        )

    def projected(h):
        snaps_in[h].wait()
        return lax.dot_general(basis_v[...], snap_v[h], CONTRACT, preferred_element_type=F32)

    basis_in.wait()
    part = projected(0)
    for h in range(2):
        xbuf[h] = part[:, h * LANES:(h + 1) * LANES]
    pl.semaphore_wait(barrier, len(peers))
    send_part = across(xbuf, ybuf, 0)
    send_part.start()
    part = projected(1)
    send_part.wait()
    mine = s // 2
    for h in range(2):
        pbuf[h] = part[:, h * LANES:(h + 1) * LANES] + ybuf[h]
        for d in (4, 3, 5, 2, 6, 1, 7, 0):
            zz = (z + d) % NZ
            to = h * NZ + zz
            copy = pltpu.make_async_remote_copy(
                src_ref=pbuf.at[h, pl.ds(pl.multiple_of(8 * zz, 8), 8)],
                dst_ref=rbuf.at[(mine - to + 16) % 16],
                send_sem=rs_send, recv_sem=rs_recv,
                device_id=(t, 2 * to + c), device_id_type=MESH,
            )
            if d == 0:
                pl.when(to != mine)(copy.start)
            else:
                copy.start()

    reg_in.wait()
    pltpu.make_async_remote_copy(
        src_ref=rbuf.at[pl.ds(1, 15)], dst_ref=rbuf.at[pl.ds(1, 15)],
        send_sem=rs_send, recv_sem=rs_recv, device_id=other, device_id_type=MESH,
    ).wait()
    zrows = pl.ds(pl.multiple_of(8 * z, 8), 8)
    total = pbuf[yl, zrows, :]
    for d in range(1, 16):
        total = total + rbuf[d]
    gbuf[me, zrows, :] = total

    def tile(zz):
        return gbuf.at[me, pl.ds(pl.multiple_of(8 * zz, 8), 8)]

    def along_z(d):
        return pltpu.make_async_remote_copy(
            src_ref=tile(z), dst_ref=tile(z), send_sem=g1_send, recv_sem=g1_recv.at[d],
            device_id=device_at(x, y, (z + d) % NZ, c), device_id_type=MESH,
        )

    def over_xy(zz):
        for dx, dy in XY_ORDER:
            pltpu.make_async_remote_copy(
                src_ref=tile(zz), dst_ref=tile(zz), send_sem=g2_send, recv_sem=g2_recv.at[4 * dx + dy],
                device_id=device_at((x + dx) % NX, (y + dy) % NY, z, c), device_id_type=MESH,
            ).start()

    for d in Z_ORDER:
        along_z(d).start()
    over_xy(z)
    for d in Z_ORDER:
        along_z(d).wait_recv()
        over_xy((z - d + NZ) % NZ)

    own = pl.ds(pl.multiple_of(c * HALF, HALF), HALF)
    send_red = across(red_ref.at[:, own], red_ref.at[:, own], 4)
    selectors(t, s, sel)
    acc[...] = jnp.zeros_like(acc)
    edge[...] = jnp.zeros_like(edge)
    edge_lane = lax.broadcasted_iota(jnp.int32, (R, LANES), 1)
    wide_lane = lax.broadcasted_iota(jnp.int32, (R, 2 * HALF), 1) % HALF
    inside = (wide_lane != 0) & (wide_lane != HALF - 1)

    def products(k, carry):
        dx = k + k // 2 - 2 * (k // 3)
        xx = (x - dx + NX) % NX
        for yy in range(NY):
            dy = (y - yy + NY) % NY
            source = 4 * xx + yy
            arrived = pltpu.make_async_remote_copy(
                src_ref=gbuf.at[source], dst_ref=gbuf.at[source], send_sem=g2_send, recv_sem=g2_recv.at[4 * dx + dy],
                device_id=other, device_id_type=MESH,
            )
            pl.when(source != me)(arrived.wait_recv)
        blocks = [gbuf[4 * xx + yy] for yy in range(NY)]

        @pl.when(k == 0)
        def _():
            red_ref[:, own] = jnp.concatenate([gbuf[2 * t], gbuf[2 * t + 1]], axis=1)
            send_red.start()

        ends = edge[...]
        for h in range(2):
            spot = 4 * (2 * (2 * xx + h) + c)
            ends = jnp.where(edge_lane // 2 == spot // 2, pltpu.roll(blocks[2 * h], spot, 1), ends)
            ends = jnp.where(edge_lane // 2 == spot // 2 + 1, pltpu.roll(blocks[2 * h + 1], spot + 4, 1), ends)
        edge[...] = ends
        pl.when(k == 3)(across(edge, oedge, 1).start)
        r = jnp.concatenate(blocks, axis=1)
        rates = jnp.where(inside, slopes(r), 0.0).astype(BF16)
        picked = jnp.dot(sel[...], split3(r), preferred_element_type=F32)
        feature = (picked[:SEL] * picked[SEL:]).astype(BF16)
        columns = jnp.concatenate([feature[ROWS_P:], rates], axis=0)
        acc[:, :ROWS_P] += lax.dot_general(columns, feature[:ROWS_P], CONTRACT, preferred_element_type=F32)
        return carry

    lax.fori_loop(0, 4, products, 0)
    theirs = pl.ds(pl.multiple_of((1 - c) * COLS_8, 8), COLS_8)
    send_norm = across(acc.at[theirs], oacc.at[pl.ds(0, COLS_8)], 2)
    send_norm.start()
    send_rhs = across(acc.at[pl.ds(COLS_P, R)], oacc.at[pl.ds(COLS_8, R)], 3)
    send_rhs.start()
    pltpu.make_async_remote_copy(
        src_ref=gbuf.at[me, pl.ds(0, 56)], dst_ref=gbuf.at[me, pl.ds(0, 56)],
        send_sem=g1_send, recv_sem=g1_recv.at[0], device_id=other, device_id_type=MESH,
    ).wait_send()
    pltpu.make_async_remote_copy(
        src_ref=gbuf.at[pl.ds(0, 15)], dst_ref=gbuf.at[pl.ds(0, 15)],
        send_sem=g2_send, recv_sem=g1_recv.at[0], device_id=other, device_id_type=MESH,
    ).wait_send()
    across(edge, oedge, 1).wait()

    ends = jnp.where(edge_lane // 4 % 2 == c, edge[...], oedge[...])
    before, after = pltpu.roll(ends, 1, 1), pltpu.roll(ends, LANES - 1, 1)
    rate = (after - before) * 0.5
    rate = jnp.where(edge_lane == 0, after - ends, rate)
    rate = jnp.where(edge_lane == 63, ends - before, rate)
    at_end = (edge_lane < 64) & ((edge_lane % 4 == 0) | (edge_lane % 4 == 3))
    rate = jnp.where(at_end, rate, 0.0)
    parts = split3(ends)
    feature = jnp.dot(sel[:ROWS_P], parts, preferred_element_type=F32)
    feature = feature * jnp.dot(sel[SEL:SEL + ROWS_P], parts, preferred_element_type=F32)
    rest = lax.dot_general(rate.astype(BF16), feature.astype(BF16), CONTRACT, preferred_element_type=F32)

    send_red.wait()
    wide_lane = lax.broadcasted_iota(jnp.int32, (R, GROUP), 1)
    rates = slopes(red_ref[...])
    first = pltpu.roll(rate, (LANES - 8 * t) % LANES, 1)
    last = pltpu.roll(rate, LANES - 1 - (8 * t + 7), 1)
    pad = jnp.zeros((R, GROUP - LANES), F32)
    rates = jnp.where(wide_lane == 0, jnp.concatenate([first, pad], axis=1), rates)
    rate_ref[...] = jnp.where(wide_lane == GROUP - 1, jnp.concatenate([pad, last], axis=1), rates)

    spot = COLS * (s % 4)
    lane = lax.broadcasted_iota(jnp.int32, (8, WIDE), 1)

    def pick_weight(i, v):
        return jnp.where(lane == spot + i, reg_s[COLS * s + i], v)

    weight = lax.fori_loop(0, COLS, pick_weight, jnp.zeros((8, WIDE), F32))
    column = lax.broadcasted_iota(jnp.int32, (COLS, ROWS), 0)
    row = lax.broadcasted_iota(jnp.int32, (COLS, ROWS), 1)
    diagonal = (ROWS * t + row) == (COLS * s + column)
    send_norm.wait()
    summed = (acc[pl.ds(pl.multiple_of(c * COLS_8, 8), COLS_8), :] + oacc[:COLS_8, :]) * (1.0 / SNAPS)
    norm_ref[...] = summed[:COLS, :ROWS] + jnp.where(diagonal, weight[0:1, :ROWS], 0.0)
    send_rhs.wait()
    summed = acc[COLS_P:, :ROWS_P] + oacc[COLS_8:, :ROWS_P] + rest
    rhs_ref[...] = summed[:, :ROWS] * (1.0 / SNAPS)


def write(red, rate, norm, rhs, red_out, rate_out, norm_out, rhs_out, sem):
    pairs = ((red, red_out), (rate, rate_out), (norm, norm_out), (rhs, rhs_out))
    copies = [pltpu.make_async_copy(a, b, sem.at[k]) for k, (a, b) in enumerate(pairs)]
    for copy in copies:
        copy.start()
    for copy in copies:
        copy.wait()


def local(snapshots, modes_basis, reg_weights):
    f32 = lambda *shape: pltpu.VMEM(shape, F32)
    bf16 = lambda *shape: pltpu.VMEM(shape, BF16)
    dma = pltpu.SemaphoreType.DMA
    shapes = ((R, GROUP), (R, GROUP), (COLS, ROWS), (R, ROWS))
    in_hbm = lambda a: pltpu.with_memory_space_constraint(a, pltpu.HBM)
    in_vmem = lambda a: pltpu.with_memory_space_constraint(a, pltpu.VMEM)
    outs = pl.pallas_call(
        kernel,
        out_shape=tuple(f32(*shape) for shape in shapes),
        in_specs=[pl.BlockSpec(memory_space=pltpu.HBM)] * 3,
        out_specs=[pl.BlockSpec(memory_space=pltpu.VMEM)] * 4,
        scratch_shapes=[
            bf16(2, HALF, 2048),
            bf16(R, 2048),
            pltpu.SMEM((FEATURES,), F32),
            f32(2, R, LANES),
            f32(2, R, LANES),
            f32(2, R, LANES),
            f32(16, 8, LANES),
            f32(16, R, LANES),
            bf16(2 * SEL, 256),
            f32(R, LANES),
            f32(R, LANES),
            f32(COLS_P + R, WIDE),
            f32(COLS_8 + R, WIDE),
            dma((4,)),
            dma, dma,
            dma, dma((NZ,)),
            dma, dma((16,)),
            dma((5,)), dma((5,)),
        ],
        compiler_params=pltpu.CompilerParams(
            collective_id=0, has_side_effects=True, vmem_limit_bytes=32 * 1024 * 1024
        ),
        cost_estimate=pl.CostEstimate(flops=1 << 30, bytes_accessed=3 << 20, transcendentals=0),
    )(in_hbm(snapshots), in_hbm(modes_basis.T), in_hbm(reg_weights))
    outs = pl.pallas_call(
        write,
        out_shape=tuple(jax.ShapeDtypeStruct(shape, F32) for shape in shapes),
        in_specs=[pl.BlockSpec(memory_space=pltpu.VMEM)] * 4,
        out_specs=[pl.BlockSpec(memory_space=pltpu.HBM)] * 4,
        scratch_shapes=[dma((4,))],
        compiler_params=pltpu.CompilerParams(vmem_limit_bytes=4 * 1024 * 1024),
    )(*[in_vmem(out) for out in outs])
    return tuple(out.T for out in outs)


def solution(mesh):
    return jax.shard_map(
        local,
        mesh=mesh,
        in_specs=(P("tm", "space"), P("space", None), P()),
        out_specs=(P("tm", None), P("tm", None), P("tm", "space"), P("tm", None)),
        check_vma=False,
    )
```

```python
import functools

import jax
import jax.numpy as jnp
from jax import lax
from jax.experimental import pallas as pl
from jax.experimental.pallas import tpu as pltpu
from jax.sharding import PartitionSpec as P

MESH = pl.DeviceIdType.MESH
F32 = jnp.float32
BF16 = jnp.bfloat16
CONTRACT = (((1,), (1,)), ((), ()))

NX, NY, NZ = 4, 4, 8
R = 64
FEATURES = 2144
SNAPS = 4096
GROUP = 512
LANES = 128
HALF = 256
ROWS = FEATURES // 8
COLS = FEATURES // 32
ROWS_P = 272
COLS_8 = 72
COLS_P = 2 * COLS_8
WIDE = 384
SEL = ROWS_P + COLS_P
XY_ORDER = [(dx, dy) for dx in (0, 1, 3, 2) for dy in (0, 1, 3, 2) if dx or dy]
Z_ORDER = (0, 1, 2, 3, 7, 4, 6, 5)
OWNERS = 2
TILE = R // OWNERS


def start_of(q):
    return R + R * q - (q * (q - 1)) // 2


def position():
    t, s = lax.axis_index("tm"), lax.axis_index("space")
    x, yh = t // 2, t % 2
    yl, z, c = s // 16, (s % 16) // 2, s % 2
    return t, s, x, yh * 2 + yl, z, c


def device_at(x, y, z, c):
    return (x * 2 + y // 2, (y % 2) * 16 + z * 2 + c)


def selectors(t, s, sel_ref):
    shape = (SEL, 256)
    row = lax.broadcasted_iota(jnp.int32, shape, 0)
    lane = lax.broadcasted_iota(jnp.int32, shape, 1)
    column = row - ROWS_P
    column = jnp.where(column < COLS_8, column, column - COLS_8 + COLS)
    f = jnp.where(row < ROWS_P, ROWS * t + row, 2 * COLS * (s // 2) + column)
    q = lane % R
    part = lane < 3 * R
    begin = start_of(q)
    linear = f < R
    first = (f >= begin) & (f < start_of(q + 1))
    first = ((linear & (f == q)) | first) & part
    count = jnp.sum(jnp.where((f >= begin) & (lane < R), 1.0, 0.0), axis=1, keepdims=True)
    i = count.astype(jnp.int32) - 1
    j = f - start_of(i) + i
    second = (linear & (lane == 3 * R)) | (~linear & (q == j) & part)
    sel_ref[:SEL, :] = jnp.where(first, 1.0, 0.0).astype(BF16)
    sel_ref[SEL:, :] = jnp.where(second, 1.0, 0.0).astype(BF16)


def split3(r):
    high = r.astype(BF16)
    rest = r - high.astype(F32)
    middle = rest.astype(BF16)
    low = (rest - middle.astype(F32)).astype(BF16)
    ones = jnp.where(lax.broadcasted_iota(jnp.int32, r.shape, 0) == 0, 1.0, 0.0).astype(BF16)
    return jnp.concatenate([high, middle, low, ones], axis=0)


def slopes(r):
    width = r.shape[1]
    return (pltpu.roll(r, width - 1, 1) - pltpu.roll(r, 1, 1)) * 0.5


def kernel(
    snap_hbm, basis_hbm, reg_hbm,
    red_ref, rate_ref, norm_ref, rhs_ref,
    snap_v, basis_v, reg_s, xbuf, ybuf, pbuf, rbuf, gbuf, sel, edge, oedge, acc, oacc,
    in_sem, rs_send, rs_recv, g1_send, g1_recv, g2_send, g2_recv, x_send, x_recv, go,
):
    t, s, x, y, z, c = position()
    yl = y % 2
    me = 4 * x + y
    other = device_at(x, y, z, 1 - c)
    partner = y // 2 * 2 + 1 - yl

    basis_in = pltpu.make_async_copy(basis_hbm, basis_v, in_sem.at[4])
    basis_in.start()
    snaps_in = []
    for k in range(4):
        core = c if k >= 2 else 1 - c
        rows = pl.ds(pl.multiple_of(core * HALF + k % 2 * LANES, LANES), LANES)
        copy = pltpu.make_async_copy(snap_hbm.at[rows], snap_v.at[k], in_sem.at[k])
        copy.start()
        snaps_in.append(copy)
    reg_in = pltpu.make_async_copy(reg_hbm, reg_s, in_sem.at[5])
    reg_in.start()

    barrier = pltpu.get_barrier_semaphore()

    def greet(chip, core):
        pl.semaphore_signal(barrier, inc=1, device_id=device_at(*chip, core), device_id_type=MESH)

    pl.when(c == 1)(lambda: greet((x, y, z), 0))

    @pl.when(z < OWNERS)
    def _():
        for d in range(1, NZ):
            for yy in (partner, y):
                greet((x, yy, (z + d) % NZ), 0)
        greet((x, partner, z), 0)

    for dx, dy in XY_ORDER:
        greet(((x + dx) % NX, (y + dy) % NY, z), 1)

    @pl.when(c == 0)
    def _():
        pl.semaphore_wait(barrier, 1 + 2 * (2 * OWNERS - 1) + 2 * (z // OWNERS > 0).astype(jnp.int32))
        pl.semaphore_signal(go, inc=1, device_id=other, device_id_type=MESH)

    def across(src, dst, k):
        return pltpu.make_async_remote_copy(
            src_ref=src, dst_ref=dst, send_sem=x_send.at[k], recv_sem=x_recv.at[k],
            device_id=other, device_id_type=MESH,
        )

    def projected(k):
        snaps_in[k].wait()
        return lax.dot_general(basis_v[...], snap_v[k], CONTRACT, preferred_element_type=F32)

    basis_in.wait()
    for h in range(2):
        xbuf[h] = projected(h)
    pl.when(c == 1)(lambda: pl.semaphore_wait(go, 1))
    send_part = across(xbuf, ybuf, 0)
    send_part.start()
    for h in range(2):
        pbuf[h] = projected(2 + h)
    send_part.wait_recv()
    mine = s // 2
    for h in range(2):
        pbuf[h] += ybuf[h]
        for zz in range(OWNERS):
            to = h * NZ + zz
            copy = pltpu.make_async_remote_copy(
                src_ref=pbuf.at[h, pl.ds(TILE * zz, TILE)], dst_ref=rbuf.at[(mine - to + 16) % 16],
                send_sem=rs_send, recv_sem=rs_recv,
                device_id=(t, 2 * to + c), device_id_type=MESH,
            )
            pl.when(to != mine)(copy.start)

    reg_in.wait()
    @pl.when(c == 1)
    def _():
        pl.semaphore_wait(barrier, 2 * (NX * NY - 1))
        pl.semaphore_signal(go, inc=1, device_id=other, device_id_type=MESH)

    pl.when(c == 0)(lambda: pl.semaphore_wait(go, 1))

    def tile(zz):
        return gbuf.at[me, pl.ds(pl.multiple_of(TILE * zz, TILE), TILE)]

    def over_xy(zz):
        for dx, dy in XY_ORDER:
            pltpu.make_async_remote_copy(
                src_ref=tile(zz), dst_ref=tile(zz), send_sem=g2_send, recv_sem=g2_recv.at[4 * dx + dy],
                device_id=device_at((x + dx) % NX, (y + dy) % NY, z, c), device_id_type=MESH,
            ).start()

    @pl.when(z < OWNERS)
    def _():
        pltpu.make_async_remote_copy(
            src_ref=rbuf.at[pl.ds(1, 15)], dst_ref=rbuf.at[pl.ds(1, 15)],
            send_sem=rs_send, recv_sem=rs_recv, device_id=other, device_id_type=MESH,
        ).wait_recv()
        rows = pl.ds(pl.multiple_of(TILE * z, TILE), TILE)
        total = pbuf[yl, rows, :]
        for d in range(1, 16):
            total = total + rbuf[d]
        gbuf[me, rows, :] = total
        for zz in Z_ORDER:
            copy = pltpu.make_async_remote_copy(
                src_ref=tile(z), dst_ref=tile(z), send_sem=g1_send, recv_sem=g1_recv.at[z],
                device_id=device_at(x, y, zz, c), device_id_type=MESH,
            )
            pl.when(zz != z)(copy.start)
        over_xy(z)

    for k in range(OWNERS):
        zz = jnp.where(z < OWNERS, z + k, jnp.where(z < 6, OWNERS - 1 - k, k)) % OWNERS

        @pl.when(zz != z)
        def _():
            pltpu.make_async_remote_copy(
                src_ref=tile(zz), dst_ref=tile(zz), send_sem=g1_send, recv_sem=g1_recv.at[zz],
                device_id=other, device_id_type=MESH,
            ).wait_recv()
            over_xy(zz)

    own = pl.ds(pl.multiple_of(c * HALF, HALF), HALF)
    send_red = across(red_ref.at[:, own], red_ref.at[:, own], 4)
    selectors(t, s, sel)
    acc[...] = jnp.zeros_like(acc)
    edge[...] = jnp.zeros_like(edge)
    edge_lane = lax.broadcasted_iota(jnp.int32, (R, LANES), 1)
    wide_lane = lax.broadcasted_iota(jnp.int32, (R, 2 * HALF), 1) % HALF
    inside = (wide_lane != 0) & (wide_lane != HALF - 1)

    def products(k, carry):
        dx = k + k // 2 - 2 * (k // 3)
        xx = (x - dx + NX) % NX
        for yy in range(NY):
            dy = (y - yy + NY) % NY
            source = 4 * xx + yy
            arrived = pltpu.make_async_remote_copy(
                src_ref=gbuf.at[source], dst_ref=gbuf.at[source], send_sem=g2_send, recv_sem=g2_recv.at[4 * dx + dy],
                device_id=other, device_id_type=MESH,
            )
            pl.when(source != me)(arrived.wait_recv)
        blocks = [gbuf[4 * xx + yy] for yy in range(NY)]

        @pl.when(k == 0)
        def _():
            red_ref[:, own] = jnp.concatenate([gbuf[2 * t], gbuf[2 * t + 1]], axis=1)
            send_red.start()

        ends = edge[...]
        for h in range(2):
            spot = 4 * (2 * (2 * xx + h) + c)
            ends = jnp.where(edge_lane // 2 == spot // 2, pltpu.roll(blocks[2 * h], spot, 1), ends)
            ends = jnp.where(edge_lane // 2 == spot // 2 + 1, pltpu.roll(blocks[2 * h + 1], spot + 4, 1), ends)
        edge[...] = ends
        pl.when(k == 3)(across(edge, oedge, 1).start)
        r = jnp.concatenate(blocks, axis=1)
        rates = jnp.where(inside, slopes(r), 0.0).astype(BF16)
        picked = jnp.dot(sel[...], split3(r), preferred_element_type=F32)
        feature = (picked[:SEL] * picked[SEL:]).astype(BF16)
        columns = jnp.concatenate([feature[ROWS_P:], rates], axis=0)
        acc[:, :ROWS_P] += lax.dot_general(columns, feature[:ROWS_P], CONTRACT, preferred_element_type=F32)
        return carry

    lax.fori_loop(0, 4, products, 0)
    theirs = pl.ds(pl.multiple_of((1 - c) * COLS_8, 8), COLS_8)
    send_norm = across(acc.at[theirs], oacc.at[pl.ds(0, COLS_8)], 2)
    send_norm.start()
    send_rhs = across(acc.at[pl.ds(COLS_P, R)], oacc.at[pl.ds(COLS_8, R)], 3)
    send_rhs.start()
    send_edge = across(edge, oedge, 1)
    send_edge.wait_recv()

    ends = jnp.where(edge_lane // 4 % 2 == c, edge[...], oedge[...])
    before, after = pltpu.roll(ends, 1, 1), pltpu.roll(ends, LANES - 1, 1)
    rate = (after - before) * 0.5
    rate = jnp.where(edge_lane == 0, after - ends, rate)
    rate = jnp.where(edge_lane == 63, ends - before, rate)
    at_end = (edge_lane < 64) & ((edge_lane % 4 == 0) | (edge_lane % 4 == 3))
    rate = jnp.where(at_end, rate, 0.0)
    parts = split3(ends)
    feature = jnp.dot(sel[:ROWS_P], parts, preferred_element_type=F32)
    feature = feature * jnp.dot(sel[SEL:SEL + ROWS_P], parts, preferred_element_type=F32)
    rest = lax.dot_general(rate.astype(BF16), feature.astype(BF16), CONTRACT, preferred_element_type=F32)

    send_red.wait_recv()
    wide_lane = lax.broadcasted_iota(jnp.int32, (R, GROUP), 1)
    rates = slopes(red_ref[...])
    first = pltpu.roll(rate, (LANES - 8 * t) % LANES, 1)
    last = pltpu.roll(rate, LANES - 1 - (8 * t + 7), 1)
    pad = jnp.zeros((R, GROUP - LANES), F32)
    rates = jnp.where(wide_lane == 0, jnp.concatenate([first, pad], axis=1), rates)
    rate_ref[...] = jnp.where(wide_lane == GROUP - 1, jnp.concatenate([pad, last], axis=1), rates)

    spot = COLS * (s % 4)
    lane = lax.broadcasted_iota(jnp.int32, (8, WIDE), 1)

    def pick_weight(i, v):
        return jnp.where(lane == spot + i, reg_s[COLS * s + i], v)

    weight = lax.fori_loop(0, COLS, pick_weight, jnp.zeros((8, WIDE), F32))
    column = lax.broadcasted_iota(jnp.int32, (COLS, ROWS), 0)
    row = lax.broadcasted_iota(jnp.int32, (COLS, ROWS), 1)
    diagonal = (ROWS * t + row) == (COLS * s + column)
    send_norm.wait_recv()
    summed = (acc[pl.ds(pl.multiple_of(c * COLS_8, 8), COLS_8), :] + oacc[:COLS_8, :]) * (1.0 / SNAPS)
    norm_ref[...] = summed[:COLS, :ROWS] + jnp.where(diagonal, weight[0:1, :ROWS], 0.0)
    send_rhs.wait_recv()
    summed = acc[COLS_P:, :ROWS_P] + oacc[COLS_8:, :ROWS_P] + rest
    rhs_ref[...] = summed[:, :ROWS] * (1.0 / SNAPS)


    def sent(ref, sem):
        pltpu.make_async_remote_copy(
            src_ref=ref, dst_ref=ref, send_sem=sem, recv_sem=g1_recv.at[0], device_id=other, device_id_type=MESH,
        ).wait_send()

    sent(gbuf.at[pl.ds(0, 15)], g2_send)
    sent(rbuf.at[pl.ds(0, 2 * OWNERS - 1)], rs_send)
    pl.when(z >= OWNERS)(lambda: sent(rbuf.at[0], rs_send))
    pl.when(z < OWNERS)(lambda: sent(rbuf.at[pl.ds(0, 7)], g1_send))
    for copy in (send_part, send_edge, send_red, send_norm, send_rhs):
        copy.wait_send()


def write(red, rate, norm, rhs, red_out, rate_out, norm_out, rhs_out, sem):
    pairs = ((red, red_out), (rate, rate_out), (norm, norm_out), (rhs, rhs_out))
    copies = [pltpu.make_async_copy(a, b, sem.at[k]) for k, (a, b) in enumerate(pairs)]
    for copy in copies:
        copy.start()
    for copy in copies:
        copy.wait()


def local(snapshots, modes_basis, reg_weights):
    f32 = lambda *shape: pltpu.VMEM(shape, F32)
    bf16 = lambda *shape: pltpu.VMEM(shape, BF16)
    dma = pltpu.SemaphoreType.DMA
    shapes = ((R, GROUP), (R, GROUP), (COLS, ROWS), (R, ROWS))
    in_hbm = lambda a: pltpu.with_memory_space_constraint(a, pltpu.HBM)
    in_vmem = lambda a: pltpu.with_memory_space_constraint(a, pltpu.VMEM)
    outs = pl.pallas_call(
        kernel,
        out_shape=tuple(f32(*shape) for shape in shapes),
        in_specs=[pl.BlockSpec(memory_space=pltpu.HBM)] * 3,
        out_specs=[pl.BlockSpec(memory_space=pltpu.VMEM)] * 4,
        scratch_shapes=[
            bf16(4, LANES, 2048),
            bf16(R, 2048),
            pltpu.SMEM((FEATURES,), F32),
            f32(2, R, LANES),
            f32(2, R, LANES),
            f32(2, R, LANES),
            f32(16, TILE, LANES),
            f32(16, R, LANES),
            bf16(2 * SEL, 256),
            f32(R, LANES),
            f32(R, LANES),
            f32(COLS_P + R, WIDE),
            f32(COLS_8 + R, WIDE),
            dma((6,)),
            dma, dma,
            dma, dma((OWNERS,)),
            dma, dma((16,)),
            dma((5,)), dma((5,)),
            pltpu.SemaphoreType.REGULAR,
        ],
        compiler_params=pltpu.CompilerParams(
            collective_id=0, has_side_effects=True, vmem_limit_bytes=32 * 1024 * 1024
        ),
        cost_estimate=pl.CostEstimate(flops=1 << 30, bytes_accessed=3 << 20, transcendentals=0),
    )(in_hbm(snapshots), in_hbm(modes_basis.T), in_hbm(reg_weights))
    outs = pl.pallas_call(
        write,
        out_shape=tuple(jax.ShapeDtypeStruct(shape, F32) for shape in shapes),
        in_specs=[pl.BlockSpec(memory_space=pltpu.VMEM)] * 4,
        out_specs=[pl.BlockSpec(memory_space=pltpu.HBM)] * 4,
        scratch_shapes=[dma((4,))],
        compiler_params=pltpu.CompilerParams(vmem_limit_bytes=4 * 1024 * 1024),
    )(*[in_vmem(out) for out in outs])
    return tuple(out.T for out in outs)


def solution(mesh):
    return jax.shard_map(
        local,
        mesh=mesh,
        in_specs=(P("tm", "space"), P("space", None), P()),
        out_specs=(P("tm", None), P("tm", None), P("tm", "space"), P("tm", None)),
        check_vma=False,
    )
```

```python
import functools

import jax
import jax.numpy as jnp
from jax import lax
from jax.experimental import pallas as pl
from jax.experimental.pallas import tpu as pltpu
from jax.sharding import PartitionSpec as P

MESH = pl.DeviceIdType.MESH
F32 = jnp.float32
BF16 = jnp.bfloat16
CONTRACT = (((1,), (1,)), ((), ()))

NX, NY, NZ = 4, 4, 8
R = 64
FEATURES = 2144
SNAPS = 4096
GROUP = 512
LANES = 128
HALF = 256
ROWS = FEATURES // 8
COLS = FEATURES // 32
ROWS_P = 272
COLS_8 = 72
COLS_P = 2 * COLS_8
WIDE = 384
SEL = ROWS_P + COLS_P
XY_ORDER = [(dx, dy) for dx in (0, 1, 3, 2) for dy in (0, 1, 3, 2) if dx or dy]
Z_ORDER = (0, 1, 2, 3, 7, 4, 6, 5)
OWNERS = 2
STRIDE = 3
TILE = R // OWNERS


def start_of(q):
    return R + R * q - (q * (q - 1)) // 2


def position():
    t, s = lax.axis_index("tm"), lax.axis_index("space")
    x, yh = t // 2, t % 2
    yl, z, c = s // 16, (s % 16) // 2, s % 2
    return t, s, x, yh * 2 + yl, z, c


def device_at(x, y, z, c):
    return (x * 2 + y // 2, (y % 2) * 16 + z * 2 + c)


def selectors(t, s, sel_ref):
    shape = (SEL, 256)
    row = lax.broadcasted_iota(jnp.int32, shape, 0)
    lane = lax.broadcasted_iota(jnp.int32, shape, 1)
    column = row - ROWS_P
    column = jnp.where(column < COLS_8, column, column - COLS_8 + COLS)
    f = jnp.where(row < ROWS_P, ROWS * t + row, 2 * COLS * (s // 2) + column)
    q = lane % R
    part = lane < 3 * R
    begin = start_of(q)
    linear = f < R
    first = (f >= begin) & (f < start_of(q + 1))
    first = ((linear & (f == q)) | first) & part
    count = jnp.sum(jnp.where((f >= begin) & (lane < R), 1.0, 0.0), axis=1, keepdims=True)
    i = count.astype(jnp.int32) - 1
    j = f - start_of(i) + i
    second = (linear & (lane == 3 * R)) | (~linear & (q == j) & part)
    sel_ref[:SEL, :] = jnp.where(first, 1.0, 0.0).astype(BF16)
    sel_ref[SEL:, :] = jnp.where(second, 1.0, 0.0).astype(BF16)


def weights(s, reg_s):
    spot = COLS * (s % 4)
    lane = lax.broadcasted_iota(jnp.int32, (8, WIDE), 1)

    def pick(i, v):
        return jnp.where(lane == spot + i, reg_s[COLS * s + i], v)

    return lax.fori_loop(0, COLS, pick, jnp.zeros((8, WIDE), F32))


def split3(r):
    high = r.astype(BF16)
    rest = r - high.astype(F32)
    middle = rest.astype(BF16)
    low = (rest - middle.astype(F32)).astype(BF16)
    ones = jnp.where(lax.broadcasted_iota(jnp.int32, r.shape, 0) == 0, 1.0, 0.0).astype(BF16)
    return jnp.concatenate([high, middle, low, ones], axis=0)


def slopes(r):
    width = r.shape[1]
    return (pltpu.roll(r, width - 1, 1) - pltpu.roll(r, 1, 1)) * 0.5


def kernel(
    snap_hbm, basis_hbm, reg_hbm,
    red_ref, rate_ref, norm_ref, rhs_ref,
    snap_v, basis_v, reg_s, xbuf, ybuf, pbuf, rbuf, gbuf, sel, edge, oedge, acc, oacc,
    in_sem, rs_send, rs_recv, g1_send, g1_recv, g2_send, g2_recv, x_send, x_recv, go,
):
    t, s, x, y, z, c = position()
    yl = y % 2
    me = 4 * x + y
    nth = z // STRIDE
    owns = (z % STRIDE == 0) & (nth < OWNERS)
    other = device_at(x, y, z, 1 - c)
    partner = y // 2 * 2 + 1 - yl

    basis_in = pltpu.make_async_copy(basis_hbm, basis_v, in_sem.at[4])
    basis_in.start()
    snaps_in = []
    for k in range(4):
        core = c if k >= 2 else 1 - c
        rows = pl.ds(pl.multiple_of(core * HALF + k % 2 * LANES, LANES), LANES)
        copy = pltpu.make_async_copy(snap_hbm.at[rows], snap_v.at[k], in_sem.at[k])
        copy.start()
        snaps_in.append(copy)
    reg_in = pltpu.make_async_copy(reg_hbm, reg_s, in_sem.at[5])
    reg_in.start()

    barrier = pltpu.get_barrier_semaphore()

    def greet(chip, core):
        pl.semaphore_signal(barrier, inc=1, device_id=device_at(*chip, core), device_id_type=MESH)

    pl.when(c == 1)(lambda: greet((x, y, z), 0))

    @pl.when(owns)
    def _():
        for d in range(1, NZ):
            for yy in (partner, y):
                greet((x, yy, (z + d) % NZ), 0)
        greet((x, partner, z), 0)

    for dx, dy in XY_ORDER:
        greet(((x + dx) % NX, (y + dy) % NY, z), 1)

    @pl.when(c == 0)
    def _():
        pl.semaphore_wait(barrier, 1 + 2 * (2 * OWNERS - 1) + 2 * (1 - owns.astype(jnp.int32)))
        pl.semaphore_signal(go, inc=1, device_id=other, device_id_type=MESH)

    def across(src, dst, k):
        return pltpu.make_async_remote_copy(
            src_ref=src, dst_ref=dst, send_sem=x_send.at[k], recv_sem=x_recv.at[k],
            device_id=other, device_id_type=MESH,
        )

    def projected(k):
        snaps_in[k].wait()
        return lax.dot_general(basis_v[...], snap_v[k], CONTRACT, preferred_element_type=F32)

    basis_in.wait()
    xbuf[0] = projected(0)
    pl.when(c == 1)(lambda: pl.semaphore_wait(go, 1))
    send_parts = [across(xbuf.at[h], ybuf.at[h], 5 * h) for h in range(2)]
    send_parts[0].start()
    xbuf[1] = projected(1)
    send_parts[1].start()
    mine = s // 2
    for h in range(2):
        part = projected(2 + h)
        send_parts[h].wait_recv()
        pbuf[h] = part + ybuf[h]
        for zz in range(OWNERS):
            to = h * NZ + STRIDE * zz
            copy = pltpu.make_async_remote_copy(
                src_ref=pbuf.at[h, pl.ds(TILE * zz, TILE)], dst_ref=rbuf.at[(mine - to + 16) % 16],
                send_sem=rs_send, recv_sem=rs_recv,
                device_id=(t, 2 * to + c), device_id_type=MESH,
            )
            pl.when(to != mine)(copy.start)

    reg_in.wait()
    selectors(t, s, sel)
    acc[...] = jnp.zeros_like(acc)
    edge[...] = jnp.zeros_like(edge)
    weight = weights(s, reg_s)

    @pl.when(c == 1)
    def _():
        pl.semaphore_wait(barrier, 2 * (NX * NY - 1))
        pl.semaphore_signal(go, inc=1, device_id=other, device_id_type=MESH)

    pl.when(c == 0)(lambda: pl.semaphore_wait(go, 1))

    def tile(zz):
        return gbuf.at[me, pl.ds(pl.multiple_of(TILE * zz, TILE), TILE)]

    def over_xy(zz):
        for dx, dy in XY_ORDER:
            pltpu.make_async_remote_copy(
                src_ref=tile(zz), dst_ref=tile(zz), send_sem=g2_send, recv_sem=g2_recv.at[4 * dx + dy],
                device_id=device_at((x + dx) % NX, (y + dy) % NY, z, c), device_id_type=MESH,
            ).start()

    @pl.when(owns)
    def _():
        pltpu.make_async_remote_copy(
            src_ref=rbuf.at[pl.ds(1, 15)], dst_ref=rbuf.at[pl.ds(1, 15)],
            send_sem=rs_send, recv_sem=rs_recv, device_id=other, device_id_type=MESH,
        ).wait_recv()
        rows = pl.ds(pl.multiple_of(TILE * nth, TILE), TILE)
        total = pbuf[yl, rows, :]
        for d in range(1, 16):
            total = total + rbuf[d]
        gbuf[me, rows, :] = total
        for zz in Z_ORDER:
            copy = pltpu.make_async_remote_copy(
                src_ref=tile(nth), dst_ref=tile(nth), send_sem=g1_send, recv_sem=g1_recv.at[nth],
                device_id=device_at(x, y, zz, c), device_id_type=MESH,
            )
            pl.when(zz != z)(copy.start)
        over_xy(nth)

    for k in range(OWNERS):
        zz = jnp.where(owns, nth + k, jnp.where((z > 1) & (z < 6), OWNERS - 1 - k, k)) % OWNERS

        @pl.when(~(owns & (zz == nth)))
        def _():
            pltpu.make_async_remote_copy(
                src_ref=tile(zz), dst_ref=tile(zz), send_sem=g1_send, recv_sem=g1_recv.at[zz],
                device_id=other, device_id_type=MESH,
            ).wait_recv()
            over_xy(zz)

    own = pl.ds(pl.multiple_of(c * HALF, HALF), HALF)
    send_red = across(red_ref.at[:, own], red_ref.at[:, own], 4)
    edge_lane = lax.broadcasted_iota(jnp.int32, (R, LANES), 1)
    wide_lane = lax.broadcasted_iota(jnp.int32, (R, 2 * HALF), 1) % HALF
    inside = (wide_lane != 0) & (wide_lane != HALF - 1)

    def products(k, carry):
        dx = k + k // 2 - 2 * (k // 3)
        xx = (x - dx + NX) % NX
        for yy in range(NY):
            dy = (y - yy + NY) % NY
            source = 4 * xx + yy
            arrived = pltpu.make_async_remote_copy(
                src_ref=gbuf.at[source], dst_ref=gbuf.at[source], send_sem=g2_send, recv_sem=g2_recv.at[4 * dx + dy],
                device_id=other, device_id_type=MESH,
            )
            pl.when(source != me)(arrived.wait_recv)
        blocks = [gbuf[4 * xx + yy] for yy in range(NY)]

        @pl.when(k == 0)
        def _():
            red_ref[:, own] = jnp.concatenate([gbuf[2 * t], gbuf[2 * t + 1]], axis=1)
            send_red.start()

        ends = edge[...]
        for h in range(2):
            spot = 4 * (2 * (2 * xx + h) + c)
            ends = jnp.where(edge_lane // 2 == spot // 2, pltpu.roll(blocks[2 * h], spot, 1), ends)
            ends = jnp.where(edge_lane // 2 == spot // 2 + 1, pltpu.roll(blocks[2 * h + 1], spot + 4, 1), ends)
        edge[...] = ends
        pl.when(k == 3)(across(edge, oedge, 1).start)
        r = jnp.concatenate(blocks, axis=1)
        rates = jnp.where(inside, slopes(r), 0.0).astype(BF16)
        picked = jnp.dot(sel[...], split3(r), preferred_element_type=F32)
        feature = (picked[:SEL] * picked[SEL:]).astype(BF16)
        columns = jnp.concatenate([feature[ROWS_P:], rates], axis=0)
        acc[:, :ROWS_P] += lax.dot_general(columns, feature[:ROWS_P], CONTRACT, preferred_element_type=F32)
        return carry

    lax.fori_loop(0, 4, products, 0)
    theirs = pl.ds(pl.multiple_of((1 - c) * COLS_8, 8), COLS_8)
    send_norm = across(acc.at[theirs], oacc.at[pl.ds(0, COLS_8)], 2)
    send_norm.start()
    send_rhs = across(acc.at[pl.ds(COLS_P, R)], oacc.at[pl.ds(COLS_8, R)], 3)
    send_rhs.start()
    send_edge = across(edge, oedge, 1)
    send_edge.wait_recv()

    ends = jnp.where(edge_lane // 4 % 2 == c, edge[...], oedge[...])
    before, after = pltpu.roll(ends, 1, 1), pltpu.roll(ends, LANES - 1, 1)
    rate = (after - before) * 0.5
    rate = jnp.where(edge_lane == 0, after - ends, rate)
    rate = jnp.where(edge_lane == 63, ends - before, rate)
    at_end = (edge_lane < 64) & ((edge_lane % 4 == 0) | (edge_lane % 4 == 3))
    rate = jnp.where(at_end, rate, 0.0)
    parts = split3(ends)
    feature = jnp.dot(sel[:ROWS_P], parts, preferred_element_type=F32)
    feature = feature * jnp.dot(sel[SEL:SEL + ROWS_P], parts, preferred_element_type=F32)
    rest = lax.dot_general(rate.astype(BF16), feature.astype(BF16), CONTRACT, preferred_element_type=F32)

    send_red.wait_recv()
    wide_lane = lax.broadcasted_iota(jnp.int32, (R, GROUP), 1)
    rates = slopes(red_ref[...])
    first = pltpu.roll(rate, (LANES - 8 * t) % LANES, 1)
    last = pltpu.roll(rate, LANES - 1 - (8 * t + 7), 1)
    pad = jnp.zeros((R, GROUP - LANES), F32)
    rates = jnp.where(wide_lane == 0, jnp.concatenate([first, pad], axis=1), rates)
    rate_ref[...] = jnp.where(wide_lane == GROUP - 1, jnp.concatenate([pad, last], axis=1), rates)

    column = lax.broadcasted_iota(jnp.int32, (COLS, ROWS), 0)
    row = lax.broadcasted_iota(jnp.int32, (COLS, ROWS), 1)
    diagonal = (ROWS * t + row) == (COLS * s + column)
    send_norm.wait_recv()
    summed = (acc[pl.ds(pl.multiple_of(c * COLS_8, 8), COLS_8), :] + oacc[:COLS_8, :]) * (1.0 / SNAPS)
    norm_ref[...] = summed[:COLS, :ROWS] + jnp.where(diagonal, weight[0:1, :ROWS], 0.0)
    send_rhs.wait_recv()
    summed = acc[COLS_P:, :ROWS_P] + oacc[COLS_8:, :ROWS_P] + rest
    rhs_ref[...] = summed[:, :ROWS] * (1.0 / SNAPS)


    def sent(ref, sem):
        pltpu.make_async_remote_copy(
            src_ref=ref, dst_ref=ref, send_sem=sem, recv_sem=g1_recv.at[0], device_id=other, device_id_type=MESH,
        ).wait_send()

    sent(gbuf.at[pl.ds(0, 15)], g2_send)
    sent(rbuf.at[pl.ds(0, 2 * OWNERS - 1)], rs_send)
    pl.when(~owns)(lambda: sent(rbuf.at[0], rs_send))
    pl.when(owns)(lambda: sent(rbuf.at[pl.ds(0, 7)], g1_send))
    for copy in (*send_parts, send_edge, send_red, send_norm, send_rhs):
        copy.wait_send()


def write(red, rate, norm, rhs, red_out, rate_out, norm_out, rhs_out, sem):
    pairs = ((red, red_out), (rate, rate_out), (norm, norm_out), (rhs, rhs_out))
    copies = [pltpu.make_async_copy(a, b, sem.at[k]) for k, (a, b) in enumerate(pairs)]
    for copy in copies:
        copy.start()
    for copy in copies:
        copy.wait()


def local(snapshots, modes_basis, reg_weights):
    f32 = lambda *shape: pltpu.VMEM(shape, F32)
    bf16 = lambda *shape: pltpu.VMEM(shape, BF16)
    dma = pltpu.SemaphoreType.DMA
    shapes = ((R, GROUP), (R, GROUP), (COLS, ROWS), (R, ROWS))
    in_hbm = lambda a: pltpu.with_memory_space_constraint(a, pltpu.HBM)
    in_vmem = lambda a: pltpu.with_memory_space_constraint(a, pltpu.VMEM)
    outs = pl.pallas_call(
        kernel,
        out_shape=tuple(f32(*shape) for shape in shapes),
        in_specs=[pl.BlockSpec(memory_space=pltpu.HBM)] * 3,
        out_specs=[pl.BlockSpec(memory_space=pltpu.VMEM)] * 4,
        scratch_shapes=[
            bf16(4, LANES, 2048),
            bf16(R, 2048),
            pltpu.SMEM((FEATURES,), F32),
            f32(2, R, LANES),
            f32(2, R, LANES),
            f32(2, R, LANES),
            f32(16, TILE, LANES),
            f32(16, R, LANES),
            bf16(2 * SEL, 256),
            f32(R, LANES),
            f32(R, LANES),
            f32(COLS_P + R, WIDE),
            f32(COLS_8 + R, WIDE),
            dma((6,)),
            dma, dma,
            dma, dma((OWNERS,)),
            dma, dma((16,)),
            dma((6,)), dma((6,)),
            pltpu.SemaphoreType.REGULAR,
        ],
        compiler_params=pltpu.CompilerParams(
            collective_id=0, has_side_effects=True, vmem_limit_bytes=32 * 1024 * 1024
        ),
        cost_estimate=pl.CostEstimate(flops=1 << 30, bytes_accessed=3 << 20, transcendentals=0),
    )(in_hbm(snapshots), in_hbm(modes_basis.T), in_hbm(reg_weights))
    outs = pl.pallas_call(
        write,
        out_shape=tuple(jax.ShapeDtypeStruct(shape, F32) for shape in shapes),
        in_specs=[pl.BlockSpec(memory_space=pltpu.VMEM)] * 4,
        out_specs=[pl.BlockSpec(memory_space=pltpu.HBM)] * 4,
        scratch_shapes=[dma((4,))],
        compiler_params=pltpu.CompilerParams(vmem_limit_bytes=4 * 1024 * 1024),
    )(*[in_vmem(out) for out in outs])
    return tuple(out.T for out in outs)


def solution(mesh):
    return jax.shard_map(
        local,
        mesh=mesh,
        in_specs=(P("tm", "space"), P("space", None), P()),
        out_specs=(P("tm", None), P("tm", None), P("tm", "space"), P("tm", None)),
        check_vma=False,
    )
```

```python
import functools

import jax
import jax.numpy as jnp
from jax import lax
from jax.experimental import pallas as pl
from jax.experimental.pallas import tpu as pltpu
from jax.sharding import PartitionSpec as P

MESH = pl.DeviceIdType.MESH
F32 = jnp.float32
BF16 = jnp.bfloat16
CONTRACT = (((1,), (1,)), ((), ()))

NX, NY, NZ = 4, 4, 8
R = 64
FEATURES = 2144
SNAPS = 4096
GROUP = 512
LANES = 128
HALF = 256
ROWS = FEATURES // 8
COLS = FEATURES // 32
ROWS_P = 272
COLS_8 = 72
COLS_P = 2 * COLS_8
WIDE = 384
SEL = ROWS_P + COLS_P
XY_ORDER = [(dx, dy) for dx in (0, 1, 3, 2) for dy in (0, 1, 3, 2) if dx or dy]
XY_TARGETS = sorted(((x, y) for x in range(NX) for y in range(NY)), key=lambda p: (2 * p[0] + 3 * p[1], p))
Z_ORDER = (0, 1, 2, 3, 7, 4, 6, 5)
OWNERS = 2
STRIDE = 3
TILE = R // OWNERS


def start_of(q):
    return R + R * q - (q * (q - 1)) // 2


def over(a, b):
    return lax.div(a, jnp.int32(b))


def rest_of(a, b):
    return lax.rem(a, jnp.int32(b))


def position():
    t, s = lax.axis_index("tm"), lax.axis_index("space")
    x, yh = over(t, 2), rest_of(t, 2)
    yl, z, c = over(s, 16), over(rest_of(s, 16), 2), rest_of(s, 2)
    return t, s, x, yh * 2 + yl, z, c


def device_at(x, y, z, c):
    return (x * 2 + over(y, 2), rest_of(y, 2) * 16 + z * 2 + c)


def selectors(t, s, sel_ref):
    shape = (SEL, 256)
    row = lax.broadcasted_iota(jnp.int32, shape, 0)
    lane = lax.broadcasted_iota(jnp.int32, shape, 1)
    column = row - ROWS_P
    column = jnp.where(column < COLS_8, column, column - COLS_8 + COLS)
    f = jnp.where(row < ROWS_P, ROWS * t + row, 2 * COLS * (s // 2) + column)
    q = lane % R
    part = lane < 3 * R
    begin = start_of(q)
    linear = f < R
    first = (f >= begin) & (f < start_of(q + 1))
    first = ((linear & (f == q)) | first) & part
    count = jnp.sum(jnp.where((f >= begin) & (lane < R), 1.0, 0.0), axis=1, keepdims=True)
    i = count.astype(jnp.int32) - 1
    j = f - start_of(i) + i
    second = (linear & (lane == 3 * R)) | (~linear & (q == j) & part)
    sel_ref[:SEL, :] = jnp.where(first, 1.0, 0.0).astype(BF16)
    sel_ref[SEL:, :] = jnp.where(second, 1.0, 0.0).astype(BF16)


def weights(s, reg_s):
    spot = COLS * (s % 4)
    lane = lax.broadcasted_iota(jnp.int32, (8, WIDE), 1)

    def pick(i, v):
        return jnp.where(lane == spot + i, reg_s[COLS * s + i], v)

    return lax.fori_loop(0, COLS, pick, jnp.zeros((8, WIDE), F32))


def split3(r):
    high = r.astype(BF16)
    rest = r - high.astype(F32)
    middle = rest.astype(BF16)
    low = (rest - middle.astype(F32)).astype(BF16)
    ones = jnp.where(lax.broadcasted_iota(jnp.int32, r.shape, 0) == 0, 1.0, 0.0).astype(BF16)
    return jnp.concatenate([high, middle, low, ones], axis=0)


def slopes(r):
    width = r.shape[1]
    return (pltpu.roll(r, width - 1, 1) - pltpu.roll(r, 1, 1)) * 0.5


def kernel(
    snap_hbm, basis_hbm, reg_hbm,
    red_ref, rate_ref, norm_ref, rhs_ref,
    snap_v, basis_v, reg_s, xbuf, ybuf, pbuf, rbuf, gbuf, sel, edge, oedge, acc, oacc,
    in_sem, rs_send, rs_recv, g1_send, g1_recv, g2_send, g2_recv, x_send, x_recv, go,
):
    t, s, x, y, z, c = position()
    yl = rest_of(y, 2)
    me = 4 * x + y
    nth = over(z, STRIDE)
    owns = (rest_of(z, STRIDE) == 0) & (nth < OWNERS)
    other = device_at(x, y, z, 1 - c)
    partner = y + 1 - 2 * yl

    basis_in = pltpu.make_async_copy(basis_hbm, basis_v, in_sem.at[4])
    basis_in.start()
    snaps_in = []
    for k in range(4):
        core = c if k >= 2 else 1 - c
        rows = pl.ds(pl.multiple_of(core * HALF + k % 2 * LANES, LANES), LANES)
        copy = pltpu.make_async_copy(snap_hbm.at[rows], snap_v.at[k], in_sem.at[k])
        copy.start()
        snaps_in.append(copy)
    reg_in = pltpu.make_async_copy(reg_hbm, reg_s, in_sem.at[5])
    reg_in.start()

    barrier = pltpu.get_barrier_semaphore()

    def greet(chip, core):
        pl.semaphore_signal(barrier, inc=1, device_id=device_at(*chip, core), device_id_type=MESH)

    pl.when(c == 1)(lambda: greet((x, y, z), 0))

    @pl.when(owns)
    def _():
        for d in range(1, NZ):
            for yy in (partner, y):
                greet((x, yy, rest_of(z + d, NZ)), 0)
        greet((x, partner, z), 0)

    for dx, dy in XY_ORDER:
        greet((rest_of(x + dx, NX), rest_of(y + dy, NY), z), 1)

    @pl.when(c == 0)
    def _():
        pl.semaphore_wait(barrier, 1 + 2 * (2 * OWNERS - 1) + 2 * (1 - owns.astype(jnp.int32)))
        pl.semaphore_signal(go, inc=1, device_id=other, device_id_type=MESH)

    def across(src, dst, k):
        return pltpu.make_async_remote_copy(
            src_ref=src, dst_ref=dst, send_sem=x_send.at[k], recv_sem=x_recv.at[k],
            device_id=other, device_id_type=MESH,
        )

    def projected(k):
        snaps_in[k].wait()
        return lax.dot_general(basis_v[...], snap_v[k], CONTRACT, preferred_element_type=F32)

    basis_in.wait()
    xbuf[0] = projected(0)
    pl.when(c == 1)(lambda: pl.semaphore_wait(go, 1))
    send_parts = [across(xbuf.at[h], ybuf.at[h], 5 * h) for h in range(2)]
    send_parts[0].start()
    xbuf[1] = projected(1)
    send_parts[1].start()
    mine = over(s, 2)
    for h in range(2):
        part = projected(2 + h)
        send_parts[h].wait_recv()
        pbuf[h] = part + ybuf[h]
        for zz in range(OWNERS):
            to = h * NZ + STRIDE * zz
            copy = pltpu.make_async_remote_copy(
                src_ref=pbuf.at[h, pl.ds(TILE * zz, TILE)], dst_ref=rbuf.at[rest_of(mine - to + 16, 16)],
                send_sem=rs_send, recv_sem=rs_recv,
                device_id=(t, 2 * to + c), device_id_type=MESH,
            )
            pl.when(to != mine)(copy.start)

    reg_in.wait()
    selectors(t, s, sel)
    acc[...] = jnp.zeros_like(acc)
    edge[...] = jnp.zeros_like(edge)
    weight = weights(s, reg_s)

    @pl.when(c == 1)
    def _():
        pl.semaphore_wait(barrier, 2 * (NX * NY - 1))
        pl.semaphore_signal(go, inc=1, device_id=other, device_id_type=MESH)

    pl.when(c == 0)(lambda: pl.semaphore_wait(go, 1))

    def tile(zz):
        return gbuf.at[me, pl.ds(pl.multiple_of(TILE * zz, TILE), TILE)]

    def over_xy(zz):
        held = tile(zz)
        for xx, yy in XY_TARGETS:
            copy = pltpu.make_async_remote_copy(
                src_ref=held, dst_ref=held, send_sem=g2_send, recv_sem=g2_recv.at[me],
                device_id=(2 * xx + yy // 2, 16 * (yy % 2) + 2 * z + c), device_id_type=MESH,
            )
            pl.when(me != 4 * xx + yy)(copy.start)

    @pl.when(owns)
    def _():
        pltpu.make_async_remote_copy(
            src_ref=rbuf.at[pl.ds(1, 15)], dst_ref=rbuf.at[pl.ds(1, 15)],
            send_sem=rs_send, recv_sem=rs_recv, device_id=other, device_id_type=MESH,
        ).wait_recv()
        rows = pl.ds(pl.multiple_of(TILE * nth, TILE), TILE)
        total = pbuf[yl, rows, :]
        for d in range(1, 16):
            total = total + rbuf[d]
        gbuf[me, rows, :] = total
        for zz in Z_ORDER:
            copy = pltpu.make_async_remote_copy(
                src_ref=tile(nth), dst_ref=tile(nth), send_sem=g1_send, recv_sem=g1_recv.at[nth],
                device_id=device_at(x, y, zz, c), device_id_type=MESH,
            )
            pl.when(zz != z)(copy.start)
        over_xy(nth)

    for k in range(OWNERS):
        zz = rest_of(jnp.where(owns, nth + k, jnp.where((z > 1) & (z < 6), OWNERS - 1 - k, k)), OWNERS)

        @pl.when(~(owns & (zz == nth)))
        def _():
            pltpu.make_async_remote_copy(
                src_ref=tile(zz), dst_ref=tile(zz), send_sem=g1_send, recv_sem=g1_recv.at[zz],
                device_id=other, device_id_type=MESH,
            ).wait_recv()
            over_xy(zz)

    own = pl.ds(pl.multiple_of(c * HALF, HALF), HALF)
    send_red = across(red_ref.at[:, own], red_ref.at[:, own], 4)
    edge_lane = lax.broadcasted_iota(jnp.int32, (R, LANES), 1)
    wide_lane = lax.broadcasted_iota(jnp.int32, (R, 2 * HALF), 1) % HALF
    inside = (wide_lane != 0) & (wide_lane != HALF - 1)

    def products(k, carry):
        xx = k
        for yy in range(NY):
            source = 4 * xx + yy
            arrived = pltpu.make_async_remote_copy(
                src_ref=gbuf.at[source], dst_ref=gbuf.at[source], send_sem=g2_send, recv_sem=g2_recv.at[source],
                device_id=other, device_id_type=MESH,
            )
            pl.when(source != me)(arrived.wait_recv)
        blocks = [gbuf[4 * xx + yy] for yy in range(NY)]

        @pl.when(xx == x)
        def _():
            red_ref[:, own] = jnp.concatenate([gbuf[2 * t], gbuf[2 * t + 1]], axis=1)
            send_red.start()

        ends = edge[...]
        for h in range(2):
            spot = 4 * (2 * (2 * xx + h) + c)
            ends = jnp.where(edge_lane // 2 == spot // 2, pltpu.roll(blocks[2 * h], spot, 1), ends)
            ends = jnp.where(edge_lane // 2 == spot // 2 + 1, pltpu.roll(blocks[2 * h + 1], spot + 4, 1), ends)
        edge[...] = ends
        pl.when(k == 3)(across(edge, oedge, 1).start)
        r = jnp.concatenate(blocks, axis=1)
        rates = jnp.where(inside, slopes(r), 0.0).astype(BF16)
        picked = jnp.dot(sel[...], split3(r), preferred_element_type=F32)
        feature = (picked[:SEL] * picked[SEL:]).astype(BF16)
        columns = jnp.concatenate([feature[ROWS_P:], rates], axis=0)
        acc[:, :ROWS_P] += lax.dot_general(columns, feature[:ROWS_P], CONTRACT, preferred_element_type=F32)
        return carry

    lax.fori_loop(0, 4, products, 0)
    theirs = pl.ds(pl.multiple_of((1 - c) * COLS_8, 8), COLS_8)
    send_norm = across(acc.at[theirs], oacc.at[pl.ds(0, COLS_8)], 2)
    send_norm.start()
    send_rhs = across(acc.at[pl.ds(COLS_P, R)], oacc.at[pl.ds(COLS_8, R)], 3)
    send_rhs.start()
    send_edge = across(edge, oedge, 1)
    send_edge.wait_recv()

    ends = jnp.where(edge_lane // 4 % 2 == c, edge[...], oedge[...])
    before, after = pltpu.roll(ends, 1, 1), pltpu.roll(ends, LANES - 1, 1)
    rate = (after - before) * 0.5
    rate = jnp.where(edge_lane == 0, after - ends, rate)
    rate = jnp.where(edge_lane == 63, ends - before, rate)
    at_end = (edge_lane < 64) & ((edge_lane % 4 == 0) | (edge_lane % 4 == 3))
    rate = jnp.where(at_end, rate, 0.0)
    parts = split3(ends)
    feature = jnp.dot(sel[:ROWS_P], parts, preferred_element_type=F32)
    feature = feature * jnp.dot(sel[SEL:SEL + ROWS_P], parts, preferred_element_type=F32)
    rest = lax.dot_general(rate.astype(BF16), feature.astype(BF16), CONTRACT, preferred_element_type=F32)

    send_red.wait_recv()
    wide_lane = lax.broadcasted_iota(jnp.int32, (R, GROUP), 1)
    rates = slopes(red_ref[...])
    first = pltpu.roll(rate, (LANES - 8 * t) % LANES, 1)
    last = pltpu.roll(rate, LANES - 1 - (8 * t + 7), 1)
    pad = jnp.zeros((R, GROUP - LANES), F32)
    rates = jnp.where(wide_lane == 0, jnp.concatenate([first, pad], axis=1), rates)
    rate_ref[...] = jnp.where(wide_lane == GROUP - 1, jnp.concatenate([pad, last], axis=1), rates)

    column = lax.broadcasted_iota(jnp.int32, (COLS, ROWS), 0)
    row = lax.broadcasted_iota(jnp.int32, (COLS, ROWS), 1)
    diagonal = (ROWS * t + row) == (COLS * s + column)
    send_norm.wait_recv()
    summed = (acc[pl.ds(pl.multiple_of(c * COLS_8, 8), COLS_8), :] + oacc[:COLS_8, :]) * (1.0 / SNAPS)
    norm_ref[...] = summed[:COLS, :ROWS] + jnp.where(diagonal, weight[0:1, :ROWS], 0.0)
    send_rhs.wait_recv()
    summed = acc[COLS_P:, :ROWS_P] + oacc[COLS_8:, :ROWS_P] + rest
    rhs_ref[...] = summed[:, :ROWS] * (1.0 / SNAPS)


    def sent(ref, sem):
        pltpu.make_async_remote_copy(
            src_ref=ref, dst_ref=ref, send_sem=sem, recv_sem=g1_recv.at[0], device_id=other, device_id_type=MESH,
        ).wait_send()

    sent(gbuf.at[pl.ds(0, 15)], g2_send)
    sent(rbuf.at[pl.ds(0, 2 * OWNERS - 1)], rs_send)
    pl.when(~owns)(lambda: sent(rbuf.at[0], rs_send))
    pl.when(owns)(lambda: sent(rbuf.at[pl.ds(0, 7)], g1_send))
    for copy in (*send_parts, send_edge, send_red, send_norm, send_rhs):
        copy.wait_send()


def write(red, rate, norm, rhs, red_out, rate_out, norm_out, rhs_out, sem):
    pairs = ((red, red_out), (rate, rate_out), (norm, norm_out), (rhs, rhs_out))
    copies = [pltpu.make_async_copy(a, b, sem.at[k]) for k, (a, b) in enumerate(pairs)]
    for copy in copies:
        copy.start()
    for copy in copies:
        copy.wait()


def local(snapshots, modes_basis, reg_weights):
    f32 = lambda *shape: pltpu.VMEM(shape, F32)
    bf16 = lambda *shape: pltpu.VMEM(shape, BF16)
    dma = pltpu.SemaphoreType.DMA
    shapes = ((R, GROUP), (R, GROUP), (COLS, ROWS), (R, ROWS))
    in_hbm = lambda a: pltpu.with_memory_space_constraint(a, pltpu.HBM)
    in_vmem = lambda a: pltpu.with_memory_space_constraint(a, pltpu.VMEM)
    outs = pl.pallas_call(
        kernel,
        out_shape=tuple(f32(*shape) for shape in shapes),
        in_specs=[pl.BlockSpec(memory_space=pltpu.HBM)] * 3,
        out_specs=[pl.BlockSpec(memory_space=pltpu.VMEM)] * 4,
        scratch_shapes=[
            bf16(4, LANES, 2048),
            bf16(R, 2048),
            pltpu.SMEM((FEATURES,), F32),
            f32(2, R, LANES),
            f32(2, R, LANES),
            f32(2, R, LANES),
            f32(16, TILE, LANES),
            f32(16, R, LANES),
            bf16(2 * SEL, 256),
            f32(R, LANES),
            f32(R, LANES),
            f32(COLS_P + R, WIDE),
            f32(COLS_8 + R, WIDE),
            dma((6,)),
            dma, dma,
            dma, dma((OWNERS,)),
            dma, dma((16,)),
            dma((6,)), dma((6,)),
            pltpu.SemaphoreType.REGULAR,
        ],
        compiler_params=pltpu.CompilerParams(
            collective_id=0, has_side_effects=True, vmem_limit_bytes=32 * 1024 * 1024
        ),
        cost_estimate=pl.CostEstimate(flops=1 << 30, bytes_accessed=3 << 20, transcendentals=0),
    )(in_hbm(snapshots), in_hbm(modes_basis.T), in_hbm(reg_weights))
    outs = pl.pallas_call(
        write,
        out_shape=tuple(jax.ShapeDtypeStruct(shape, F32) for shape in shapes),
        in_specs=[pl.BlockSpec(memory_space=pltpu.VMEM)] * 4,
        out_specs=[pl.BlockSpec(memory_space=pltpu.HBM)] * 4,
        scratch_shapes=[dma((4,))],
        compiler_params=pltpu.CompilerParams(vmem_limit_bytes=4 * 1024 * 1024),
    )(*[in_vmem(out) for out in outs])
    return tuple(out.T for out in outs)


def solution(mesh):
    return jax.shard_map(
        local,
        mesh=mesh,
        in_specs=(P("tm", "space"), P("space", None), P()),
        out_specs=(P("tm", None), P("tm", None), P("tm", "space"), P("tm", None)),
        check_vma=False,
    )
```

```python
import functools

import jax
import jax.numpy as jnp
from jax import lax
from jax.experimental import pallas as pl
from jax.experimental.pallas import tpu as pltpu
from jax.sharding import PartitionSpec as P

MESH = pl.DeviceIdType.MESH
F32 = jnp.float32
BF16 = jnp.bfloat16
CONTRACT = (((1,), (1,)), ((), ()))

NX, NY, NZ = 4, 4, 8
R = 64
FEATURES = 2144
SNAPS = 4096
GROUP = 512
LANES = 128
HALF = 256
ROWS = FEATURES // 8
COLS = FEATURES // 32
ROWS_P = 272
COLS_8 = 72
COLS_P = 2 * COLS_8
WIDE = 384
SEL = ROWS_P + COLS_P
XY_ORDER = [(dx, dy) for dx in (0, 1, 3, 2) for dy in (0, 1, 3, 2) if dx or dy]
XY_TARGETS = sorted(((x, y) for x in range(NX) for y in range(NY)), key=lambda p: (p[1] + (p[0] > 0), p))
Z_ORDER = (0, 1, 2, 3, 7, 4, 6, 5)
OWNERS = 2
STRIDE = 3
TILE = R // OWNERS


def start_of(q):
    return R + R * q - (q * (q - 1)) // 2


def over(a, b):
    return lax.div(a, jnp.int32(b))


def rest_of(a, b):
    return lax.rem(a, jnp.int32(b))


def position():
    t, s = lax.axis_index("tm"), lax.axis_index("space")
    x, yh = over(t, 2), rest_of(t, 2)
    yl, z, c = over(s, 16), over(rest_of(s, 16), 2), rest_of(s, 2)
    return t, s, x, yh * 2 + yl, z, c


def device_at(x, y, z, c):
    return (x * 2 + over(y, 2), rest_of(y, 2) * 16 + z * 2 + c)


def selectors(t, s, sel_ref):
    shape = (SEL, 256)
    row = lax.broadcasted_iota(jnp.int32, shape, 0)
    lane = lax.broadcasted_iota(jnp.int32, shape, 1)
    column = row - ROWS_P
    column = jnp.where(column < COLS_8, column, column - COLS_8 + COLS)
    f = jnp.where(row < ROWS_P, ROWS * t + row, 2 * COLS * (s // 2) + column)
    q = lane % R
    part = lane < 3 * R
    begin = start_of(q)
    linear = f < R
    first = (f >= begin) & (f < start_of(q + 1))
    first = ((linear & (f == q)) | first) & part
    count = jnp.sum(jnp.where((f >= begin) & (lane < R), 1.0, 0.0), axis=1, keepdims=True)
    i = count.astype(jnp.int32) - 1
    j = f - start_of(i) + i
    second = (linear & (lane == 3 * R)) | (~linear & (q == j) & part)
    sel_ref[:SEL, :] = jnp.where(first, 1.0, 0.0).astype(BF16)
    sel_ref[SEL:, :] = jnp.where(second, 1.0, 0.0).astype(BF16)


def weights(s, reg_s):
    spot = COLS * (s % 4)
    lane = lax.broadcasted_iota(jnp.int32, (8, WIDE), 1)

    def pick(i, v):
        return jnp.where(lane == spot + i, reg_s[COLS * s + i], v)

    return lax.fori_loop(0, COLS, pick, jnp.zeros((8, WIDE), F32))


def split3(r):
    high = r.astype(BF16)
    rest = r - high.astype(F32)
    middle = rest.astype(BF16)
    low = (rest - middle.astype(F32)).astype(BF16)
    ones = jnp.where(lax.broadcasted_iota(jnp.int32, r.shape, 0) == 0, 1.0, 0.0).astype(BF16)
    return jnp.concatenate([high, middle, low, ones], axis=0)


def slopes(r):
    width = r.shape[1]
    return (pltpu.roll(r, width - 1, 1) - pltpu.roll(r, 1, 1)) * 0.5


def kernel(
    snap_hbm, basis_hbm, reg_hbm,
    red_ref, rate_ref, norm_ref, rhs_ref,
    snap_v, basis_v, reg_s, xbuf, ybuf, pbuf, rbuf, gbuf, sel, edge, oedge, acc, oacc,
    in_sem, rs_send, rs_recv, g1_send, g1_recv, g2_send, g2_recv, x_send, x_recv, go,
):
    t, s, x, y, z, c = position()
    yl = rest_of(y, 2)
    me = 4 * x + y
    nth = over(z, STRIDE)
    owns = (rest_of(z, STRIDE) == 0) & (nth < OWNERS)
    other = device_at(x, y, z, 1 - c)
    partner = y + 1 - 2 * yl

    basis_in = pltpu.make_async_copy(basis_hbm, basis_v, in_sem.at[4])
    basis_in.start()
    snaps_in = []
    for k in range(4):
        core = c if k >= 2 else 1 - c
        rows = pl.ds(pl.multiple_of(core * HALF + k % 2 * LANES, LANES), LANES)
        copy = pltpu.make_async_copy(snap_hbm.at[rows], snap_v.at[k], in_sem.at[k])
        copy.start()
        snaps_in.append(copy)
    reg_in = pltpu.make_async_copy(reg_hbm, reg_s, in_sem.at[5])
    reg_in.start()

    barrier = pltpu.get_barrier_semaphore()

    def greet(chip, core):
        pl.semaphore_signal(barrier, inc=1, device_id=device_at(*chip, core), device_id_type=MESH)

    pl.when(c == 1)(lambda: greet((x, y, z), 0))

    @pl.when(owns)
    def _():
        for d in range(1, NZ):
            for yy in (partner, y):
                greet((x, yy, rest_of(z + d, NZ)), 0)
        greet((x, partner, z), 0)

    for dx, dy in XY_ORDER:
        greet((rest_of(x + dx, NX), rest_of(y + dy, NY), z), 1)

    @pl.when(c == 0)
    def _():
        pl.semaphore_wait(barrier, 1 + 2 * (2 * OWNERS - 1) + 2 * (1 - owns.astype(jnp.int32)))
        pl.semaphore_signal(go, inc=1, device_id=other, device_id_type=MESH)

    def across(src, dst, k):
        return pltpu.make_async_remote_copy(
            src_ref=src, dst_ref=dst, send_sem=x_send.at[k], recv_sem=x_recv.at[k],
            device_id=other, device_id_type=MESH,
        )

    def projected(k):
        snaps_in[k].wait()
        return lax.dot_general(basis_v[...], snap_v[k], CONTRACT, preferred_element_type=F32)

    basis_in.wait()
    xbuf[0] = projected(0)
    pl.when(c == 1)(lambda: pl.semaphore_wait(go, 1))
    send_parts = [across(xbuf.at[h], ybuf.at[h], 5 * h) for h in range(2)]
    send_parts[0].start()
    xbuf[1] = projected(1)
    send_parts[1].start()
    mine = over(s, 2)
    for h in range(2):
        part = projected(2 + h)
        send_parts[h].wait_recv()
        pbuf[h] = part + ybuf[h]
        for zz in range(OWNERS):
            to = h * NZ + STRIDE * zz
            copy = pltpu.make_async_remote_copy(
                src_ref=pbuf.at[h, pl.ds(TILE * zz, TILE)], dst_ref=rbuf.at[rest_of(mine - to + 16, 16)],
                send_sem=rs_send, recv_sem=rs_recv,
                device_id=(t, 2 * to + c), device_id_type=MESH,
            )
            pl.when(to != mine)(copy.start)

    reg_in.wait()
    selectors(t, s, sel)
    acc[...] = jnp.zeros_like(acc)
    edge[...] = jnp.zeros_like(edge)
    weight = weights(s, reg_s)

    @pl.when(c == 1)
    def _():
        pl.semaphore_wait(barrier, 2 * (NX * NY - 1))
        pl.semaphore_signal(go, inc=1, device_id=other, device_id_type=MESH)

    pl.when(c == 0)(lambda: pl.semaphore_wait(go, 1))

    def tile(zz):
        return gbuf.at[me, pl.ds(pl.multiple_of(TILE * zz, TILE), TILE)]

    def over_xy(zz):
        held = tile(zz)
        for xx, yy in XY_TARGETS:
            copy = pltpu.make_async_remote_copy(
                src_ref=held, dst_ref=held, send_sem=g2_send, recv_sem=g2_recv.at[me],
                device_id=(2 * xx + yy // 2, 16 * (yy % 2) + 2 * z + c), device_id_type=MESH,
            )
            pl.when(me != 4 * xx + yy)(copy.start)

    @pl.when(owns)
    def _():
        pltpu.make_async_remote_copy(
            src_ref=rbuf.at[pl.ds(1, 15)], dst_ref=rbuf.at[pl.ds(1, 15)],
            send_sem=rs_send, recv_sem=rs_recv, device_id=other, device_id_type=MESH,
        ).wait_recv()
        rows = pl.ds(pl.multiple_of(TILE * nth, TILE), TILE)
        total = pbuf[yl, rows, :]
        for d in range(1, 16):
            total = total + rbuf[d]
        gbuf[me, rows, :] = total
        for zz in Z_ORDER:
            copy = pltpu.make_async_remote_copy(
                src_ref=tile(nth), dst_ref=tile(nth), send_sem=g1_send, recv_sem=g1_recv.at[nth],
                device_id=device_at(x, y, zz, c), device_id_type=MESH,
            )
            pl.when(zz != z)(copy.start)
        over_xy(nth)

    for k in range(OWNERS):
        zz = rest_of(jnp.where(owns, nth + k, jnp.where((z > 1) & (z < 6), OWNERS - 1 - k, k)), OWNERS)

        @pl.when(~(owns & (zz == nth)))
        def _():
            pltpu.make_async_remote_copy(
                src_ref=tile(zz), dst_ref=tile(zz), send_sem=g1_send, recv_sem=g1_recv.at[zz],
                device_id=other, device_id_type=MESH,
            ).wait_recv()
            over_xy(zz)

    own = pl.ds(pl.multiple_of(c * HALF, HALF), HALF)
    send_red = across(red_ref.at[:, own], red_ref.at[:, own], 4)
    edge_lane = lax.broadcasted_iota(jnp.int32, (R, LANES), 1)
    wide_lane = lax.broadcasted_iota(jnp.int32, (R, 2 * HALF), 1) % HALF
    inside = (wide_lane != 0) & (wide_lane != HALF - 1)

    def products(k, carry):
        xx = k + over(k, 2) - 2 * over(k, 3)
        for yy in range(NY):
            source = 4 * xx + yy
            arrived = pltpu.make_async_remote_copy(
                src_ref=gbuf.at[source], dst_ref=gbuf.at[source], send_sem=g2_send, recv_sem=g2_recv.at[source],
                device_id=other, device_id_type=MESH,
            )
            pl.when(source != me)(arrived.wait_recv)
        blocks = [gbuf[4 * xx + yy] for yy in range(NY)]

        @pl.when(xx == x)
        def _():
            red_ref[:, own] = jnp.concatenate([gbuf[2 * t], gbuf[2 * t + 1]], axis=1)
            send_red.start()

        ends = edge[...]
        for h in range(2):
            spot = 4 * (2 * (2 * xx + h) + c)
            ends = jnp.where(edge_lane // 2 == spot // 2, pltpu.roll(blocks[2 * h], spot, 1), ends)
            ends = jnp.where(edge_lane // 2 == spot // 2 + 1, pltpu.roll(blocks[2 * h + 1], spot + 4, 1), ends)
        edge[...] = ends
        pl.when(k == 3)(across(edge, oedge, 1).start)
        r = jnp.concatenate(blocks, axis=1)
        rates = jnp.where(inside, slopes(r), 0.0).astype(BF16)
        picked = jnp.dot(sel[...], split3(r), preferred_element_type=F32)
        feature = (picked[:SEL] * picked[SEL:]).astype(BF16)
        columns = jnp.concatenate([feature[ROWS_P:], rates], axis=0)
        acc[:, :ROWS_P] += lax.dot_general(columns, feature[:ROWS_P], CONTRACT, preferred_element_type=F32)
        return carry

    lax.fori_loop(0, 4, products, 0)
    theirs = pl.ds(pl.multiple_of((1 - c) * COLS_8, 8), COLS_8)
    send_norm = across(acc.at[theirs], oacc.at[pl.ds(0, COLS_8)], 2)
    send_norm.start()
    send_rhs = across(acc.at[pl.ds(COLS_P, R)], oacc.at[pl.ds(COLS_8, R)], 3)
    send_rhs.start()
    send_edge = across(edge, oedge, 1)
    send_edge.wait_recv()

    ends = jnp.where(edge_lane // 4 % 2 == c, edge[...], oedge[...])
    before, after = pltpu.roll(ends, 1, 1), pltpu.roll(ends, LANES - 1, 1)
    rate = (after - before) * 0.5
    rate = jnp.where(edge_lane == 0, after - ends, rate)
    rate = jnp.where(edge_lane == 63, ends - before, rate)
    at_end = (edge_lane < 64) & ((edge_lane % 4 == 0) | (edge_lane % 4 == 3))
    rate = jnp.where(at_end, rate, 0.0)
    parts = split3(ends)
    feature = jnp.dot(sel[:ROWS_P], parts, preferred_element_type=F32)
    feature = feature * jnp.dot(sel[SEL:SEL + ROWS_P], parts, preferred_element_type=F32)
    rest = lax.dot_general(rate.astype(BF16), feature.astype(BF16), CONTRACT, preferred_element_type=F32)

    send_red.wait_recv()
    wide_lane = lax.broadcasted_iota(jnp.int32, (R, GROUP), 1)
    rates = slopes(red_ref[...])
    first = pltpu.roll(rate, (LANES - 8 * t) % LANES, 1)
    last = pltpu.roll(rate, LANES - 1 - (8 * t + 7), 1)
    pad = jnp.zeros((R, GROUP - LANES), F32)
    rates = jnp.where(wide_lane == 0, jnp.concatenate([first, pad], axis=1), rates)
    rate_ref[...] = jnp.where(wide_lane == GROUP - 1, jnp.concatenate([pad, last], axis=1), rates)

    column = lax.broadcasted_iota(jnp.int32, (COLS, ROWS), 0)
    row = lax.broadcasted_iota(jnp.int32, (COLS, ROWS), 1)
    diagonal = (ROWS * t + row) == (COLS * s + column)
    send_norm.wait_recv()
    summed = (acc[pl.ds(pl.multiple_of(c * COLS_8, 8), COLS_8), :] + oacc[:COLS_8, :]) * (1.0 / SNAPS)
    norm_ref[...] = summed[:COLS, :ROWS] + jnp.where(diagonal, weight[0:1, :ROWS], 0.0)
    send_rhs.wait_recv()
    summed = acc[COLS_P:, :ROWS_P] + oacc[COLS_8:, :ROWS_P] + rest
    rhs_ref[...] = summed[:, :ROWS] * (1.0 / SNAPS)


    def sent(ref, sem):
        pltpu.make_async_remote_copy(
            src_ref=ref, dst_ref=ref, send_sem=sem, recv_sem=g1_recv.at[0], device_id=other, device_id_type=MESH,
        ).wait_send()

    sent(gbuf.at[pl.ds(0, 15)], g2_send)
    sent(rbuf.at[pl.ds(0, 2 * OWNERS - 1)], rs_send)
    pl.when(~owns)(lambda: sent(rbuf.at[0], rs_send))
    pl.when(owns)(lambda: sent(rbuf.at[pl.ds(0, 7)], g1_send))
    for copy in (*send_parts, send_edge, send_red, send_norm, send_rhs):
        copy.wait_send()


def write(red, rate, norm, rhs, red_out, rate_out, norm_out, rhs_out, sem):
    pairs = ((red, red_out), (rate, rate_out), (norm, norm_out), (rhs, rhs_out))
    copies = [pltpu.make_async_copy(a, b, sem.at[k]) for k, (a, b) in enumerate(pairs)]
    for copy in copies:
        copy.start()
    for copy in copies:
        copy.wait()


def local(snapshots, modes_basis, reg_weights):
    f32 = lambda *shape: pltpu.VMEM(shape, F32)
    bf16 = lambda *shape: pltpu.VMEM(shape, BF16)
    dma = pltpu.SemaphoreType.DMA
    shapes = ((R, GROUP), (R, GROUP), (COLS, ROWS), (R, ROWS))
    in_hbm = lambda a: pltpu.with_memory_space_constraint(a, pltpu.HBM)
    in_vmem = lambda a: pltpu.with_memory_space_constraint(a, pltpu.VMEM)
    outs = pl.pallas_call(
        kernel,
        out_shape=tuple(f32(*shape) for shape in shapes),
        in_specs=[pl.BlockSpec(memory_space=pltpu.HBM)] * 3,
        out_specs=[pl.BlockSpec(memory_space=pltpu.VMEM)] * 4,
        scratch_shapes=[
            bf16(4, LANES, 2048),
            bf16(R, 2048),
            pltpu.SMEM((FEATURES,), F32),
            f32(2, R, LANES),
            f32(2, R, LANES),
            f32(2, R, LANES),
            f32(16, TILE, LANES),
            f32(16, R, LANES),
            bf16(2 * SEL, 256),
            f32(R, LANES),
            f32(R, LANES),
            f32(COLS_P + R, WIDE),
            f32(COLS_8 + R, WIDE),
            dma((6,)),
            dma, dma,
            dma, dma((OWNERS,)),
            dma, dma((16,)),
            dma((6,)), dma((6,)),
            pltpu.SemaphoreType.REGULAR,
        ],
        compiler_params=pltpu.CompilerParams(
            collective_id=0, has_side_effects=True, vmem_limit_bytes=32 * 1024 * 1024
        ),
        cost_estimate=pl.CostEstimate(flops=1 << 30, bytes_accessed=3 << 20, transcendentals=0),
    )(in_hbm(snapshots), in_hbm(modes_basis.T), in_hbm(reg_weights))
    outs = pl.pallas_call(
        write,
        out_shape=tuple(jax.ShapeDtypeStruct(shape, F32) for shape in shapes),
        in_specs=[pl.BlockSpec(memory_space=pltpu.VMEM)] * 4,
        out_specs=[pl.BlockSpec(memory_space=pltpu.HBM)] * 4,
        scratch_shapes=[dma((4,))],
        compiler_params=pltpu.CompilerParams(vmem_limit_bytes=4 * 1024 * 1024),
    )(*[in_vmem(out) for out in outs])
    return tuple(out.T for out in outs)


def solution(mesh):
    return jax.shard_map(
        local,
        mesh=mesh,
        in_specs=(P("tm", "space"), P("space", None), P()),
        out_specs=(P("tm", None), P("tm", None), P("tm", "space"), P("tm", None)),
        check_vma=False,
    )
```
